32 devices in a mesh: dp: 4 (over x, core), inner: 2 (over y), outer: 4 (over z).
Axes of the slice: x: 2, y: 2, z: 4, core: 2. Of those that a mesh axis runs over, the one named last changes fastest.
Arguments:
- partials: bfloat16 [32, 120, 16384], P(('dp', 'inner', 'outer')), parts along dimension 0, may hold values from -5 to 5
- residual: bfloat16 [480, 16384], P('dp', ('inner', 'outer')), parts along dimension 0, may hold values from -18 to 18
- norm_gain: float32 [16384], replicated, may hold values from 0.25 to 1.75
- kv_weight: bfloat16 [16384, 8, 256], P(None, ('inner', 'outer')), may hold values from -0.046875 to 0.046875
Outputs:
- stream: bfloat16 [480, 16384], P('dp', ('inner', 'outer')), parts along dimension 0
- kv_pair: bfloat16 [480, 8, 256], P('dp', ('inner', 'outer')), parts along dimension 0
The draws below stay inside these ranges and needn't reach their ends.
There are 4 independent parts, one for each index of `dp`. The reference program is written for one: setup_inputs(seed, part) draws one part's arguments, and reference() takes and returns one part's arrays. A program takes and returns all parts, laid end to end along the dimension named above; an argument that names none is the same for every part. Nothing has to cross between parts.
All inputs are finite; a program needn't handle non-finite values.
Results may differ from the reference program's by a relative error of at most 0.015.
Values may be sent and summed in bfloat16 or wider, within the bound.
A program may use at most 128 MiB of HBM per device.

```python
import jax
import jax.numpy as jnp
from jax import lax

D = 16384
KV_HEADS = 8
HEAD = 128
SPAN = 120
TP = 8
N_INNER = 2
N_OUTER = 4


def draw_residual(key, part):
    key = jax.random.fold_in(key, 7)
    column = jnp.arange(D, dtype=jnp.float32) / (D - 1)
    spread = 0.3 * jnp.power(10.0, column)
    base = jnp.clip(jax.random.normal(key, (SPAN, D), jnp.float32), -6.0, 6.0)
    return (base * spread[None, :]).astype(jnp.bfloat16)


def with_spikes(values, stream_key, source, target, blocks, factor):
    owner, partner = [(jnp.arange(values.shape[axis_at]) // (values.shape[axis_at] // blocks)).reshape([-1 if axis == axis_at else 1 for axis in range(values.ndim)]) for axis_at in (source, target)]
    chosen = jax.random.permutation(stream_key, blocks)[partner]
    strong = (owner == chosen) | (owner == (partner + blocks // 2) % blocks)
    return jnp.where(strong, factor * values, values)


def shard_levels(key, extent, split, low, high):
    level = 1.0
    for position, shards_of in split:
        steps = jax.random.uniform(jax.random.fold_in(jax.random.fold_in(key, 6), position), (shards_of,), jnp.float32, low / len(split), high / len(split))
        level = level * jnp.repeat(jnp.exp(steps), extent[position] // shards_of).reshape((-1,) + (1,) * (len(extent) - 1 - position))
    return level


def normal_values(rng, dims, scale, bound, pieces=(), kind=jnp.bfloat16):
    level = shard_levels(rng, dims, pieces, -0.22, 0.18) if pieces else 1.0
    drawn = jax.random.normal(rng, dims, jnp.float32) * scale * level
    return jnp.minimum(jnp.maximum(drawn, -bound), bound).astype(kind)


def noise_with(key, dims, scale, most, split, heavy, kind=jnp.bfloat16):
    values = scale * jax.random.normal(key, dims, jnp.float32)
    if split:
        values = values * shard_levels(key, dims, split, -0.22, 0.18)
    return jnp.clip(with_spikes(values, jax.random.fold_in(key, 3), *heavy), -most, most).astype(kind)


def setup_inputs(seed: int = 0, part: int = 0) -> dict:
    key_of = jax.random.split(jax.random.key(seed), 5)
    part_keys = jax.random.split(jax.random.fold_in(key_of[4], part), 5)
    partials = noise_with(part_keys[0], (TP, SPAN, D), 0.25, 5.0, ((0, 8),), (0, 2, 8, 2.0))
    residual = draw_residual(jax.random.fold_in(jax.random.fold_in(key_of[4], part), 71), part)
    norm_gain = jnp.clip(1.0 + 0.15 * jax.random.normal(key_of[2], (D,), jnp.float32), 0.25, 1.75)
    kv_weight = normal_values(key_of[3], (D, KV_HEADS, 2 * HEAD), D ** -0.5, 0.046875, ((1, 8),))
    return dict(partials=partials, residual=residual, norm_gain=norm_gain, kv_weight=kv_weight)


def reference(partials, residual, norm_gain, kv_weight):
    grouped = partials.astype(jnp.float32).reshape(N_INNER, N_OUTER, SPAN, D)
    level_one = lax.optimization_barrier(jnp.sum(grouped, axis=0)).astype(jnp.bfloat16)
    level_one = lax.optimization_barrier(level_one).astype(jnp.float32)
    level_two = lax.optimization_barrier(jnp.sum(level_one, axis=0))
    stream = (residual.astype(jnp.float32) + level_two).astype(jnp.bfloat16)
    values = stream.astype(jnp.float32)
    factor = lax.rsqrt(lax.optimization_barrier(jnp.mean(values * values, axis=1)) + 1e-05)
    normed = (values * factor[:, None] * norm_gain[None, :]).astype(jnp.bfloat16)
    flat = kv_weight.reshape(D, KV_HEADS * 2 * HEAD)
    kv_pair = jnp.dot(normed, flat, preferred_element_type=jnp.float32).astype(jnp.bfloat16)
    return (stream, kv_pair.reshape(SPAN, KV_HEADS, 2 * HEAD))
```

```python
import functools

import jax
import jax.numpy as jnp
from jax import lax
from jax.experimental import pallas as pl
from jax.experimental.pallas import tpu as pltpu
from jax.sharding import PartitionSpec as P

MESH = pl.DeviceIdType.MESH
F32 = jnp.float32
BF16 = jnp.bfloat16
PIECES = 8
AHEAD = 2


def fused(n, pieces, partials, residual, gain, weight, stream_out, kv_out,
          mine, resid, gains, w, ybuf, rbuf, lbuf, ga, gb, tmp, acc, sq,
          loc, y_s, y_r, r_s, r_r, l_s, l_r, a_r, a_rs, a_ls, a_ys,
          b_r, b_rs, b_ls, b_ys):
    i = lax.axis_index("inner")
    o = lax.axis_index("outer")
    other = 1 - i
    rows, local = resid.shape
    width = gains.shape[1]
    half = n * local
    cols = local // pieces
    cut = cols // 2
    to_y = {"inner": other}
    to_r = {"outer": jnp.minimum(o + 1, n - 1)}
    to_l = {"outer": jnp.maximum(o - 1, 0)}
    has_r = o < n - 1
    has_l = o > 0

    loads = [
        pltpu.make_async_copy(
            partials.at[0, :, pl.ds(pl.multiple_of(i * half, half), half)], mine, loc.at[0]
        ),
        pltpu.make_async_copy(residual, resid, loc.at[1]),
        pltpu.make_async_copy(gain, gains, loc.at[2]),
        pltpu.make_async_copy(weight, w, loc.at[3]),
    ]

    def remote(src, dst, ssem, rsem, to):
        return pltpu.make_async_remote_copy(
            src_ref=src, dst_ref=dst, send_sem=ssem, recv_sem=rsem,
            device_id=to, device_id_type=MESH,
        )

    def y_copy(d, p):
        at = pl.multiple_of(other * half + d * local + p * cols, cols)
        return remote(partials.at[0, :, pl.ds(at, cols)], ybuf.at[d, p],
                      y_s.at[d, p], y_r.at[d, p], to_y)

    def r_copy(d, p):
        return remote(rbuf.at[d, p], rbuf.at[d, p], r_s.at[d, p], r_r.at[d, p], to_r)

    def l_copy(d, p):
        return remote(lbuf.at[d, p], lbuf.at[d, p], l_s.at[d, p], l_r.at[d, p], to_l)

    def a_copy(c, p, ssem, to):
        t = i * n + c
        return remote(ga.at[t, p], ga.at[t, p], ssem.at[c, p], a_r.at[t, p], to)

    def b_copy(t, p, ssem, to):
        return remote(gb.at[t, p], gb.at[t, p], ssem, b_r.at[t, p], to)

    def inside(p):
        return (p >= 0) & (p < pieces)

    def level_one(d, p):
        y_copy(d, p).wait_recv()
        at = pl.multiple_of(d * local + p * cols, cols)
        return mine[:, pl.ds(at, cols)].astype(F32) + ybuf[d, p].astype(F32)

    def skew(d):
        return jnp.where(d > o, o, jnp.where(d < o, n - 1 - o, n - 1))

    def send_y(s):
        for d in range(n):
            p = s - skew(d)

            @pl.when(inside(p))
            def _():
                y_copy(d, p).start()

    barrier = pltpu.get_barrier_semaphore()
    pl.semaphore_signal(barrier, inc=1, device_id=to_y, device_id_type=MESH)

    @pl.when(has_r)
    def _():
        pl.semaphore_signal(barrier, inc=1, device_id=to_r, device_id_type=MESH)

    @pl.when(has_l)
    def _():
        pl.semaphore_signal(barrier, inc=1, device_id=to_l, device_id_type=MESH)

    pl.semaphore_wait(barrier, 1 + has_r.astype(jnp.int32) + has_l.astype(jnp.int32))
    for s in range(AHEAD):
        send_y(jnp.int32(s))
    for load in loads:
        load.start()
    acc[...] = jnp.zeros_like(acc)
    sq[...] = jnp.zeros_like(sq)
    for load in loads[:3]:
        load.wait()

    def passing(s):
        p = s - o

        @pl.when(inside(p) & has_r)
        def _():
            for d in reversed(range(n)):
                @pl.when(d > o)
                def _():
                    value = level_one(d, p)

                    @pl.when(has_l)
                    def _():
                        r_copy(d, p).wait_recv()
                        rbuf[d, p] = (value + rbuf[d, p].astype(F32)).astype(BF16)

                    @pl.when(jnp.logical_not(has_l))
                    def _():
                        rbuf[d, p] = value.astype(BF16)

                    r_copy(d, p).start()

        q = s - (n - 1 - o)

        @pl.when(inside(q) & has_l)
        def _():
            for d in range(n):
                @pl.when(d < o)
                def _():
                    value = level_one(d, q)

                    @pl.when(has_r)
                    def _():
                        l_copy(d, q).wait_recv()
                        lbuf[d, q] = (value + lbuf[d, q].astype(F32)).astype(BF16)

                    @pl.when(jnp.logical_not(has_r))
                    def _():
                        lbuf[d, q] = value.astype(BF16)

                    l_copy(d, q).start()

    def finish(s):
        p = s - (n - 1)

        @pl.when(inside(p))
        def _():
            at = pl.multiple_of(p * cols, cols)
            tmp[...] = level_one(o, p) + resid[:, pl.ds(at, cols)].astype(F32)

            @pl.when(has_l)
            def _():
                r_copy(o, p).wait_recv()
                tmp[...] += rbuf[o, p].astype(F32)

            @pl.when(has_r)
            def _():
                l_copy(o, p).wait_recv()
                tmp[...] += lbuf[o, p].astype(F32)

            value = tmp[...].astype(BF16)
            stream_out[:, pl.ds(at, cols)] = value
            me = i * n + o
            ga[me, p] = value[:, :cut]
            gb[me, p] = value[:, cut:]
            b_copy(me, p, b_ys.at[p], to_y).start()

    def spread(s, far):
        for c in range(n):
            p = s - (n - 1) - jnp.abs(o - c) - far
            t = (other if far else i) * n + c

            @pl.when(inside(p))
            def _():
                if far:
                    a_in = remote(ga.at[t, p], ga.at[t, p], a_ys.at[c, p], a_r.at[t, p], to_y)
                    a_in.wait_recv()
                    b_copy(t, p, b_ys.at[p], to_y).wait_recv()
                else:
                    @pl.when(c != o)
                    def _():
                        a_copy(c, p, a_ys, to_y).wait_recv()
                        b_copy(t, p, b_ys.at[p], to_y).wait_recv()
                    a_copy(c, p, a_ys, to_y).start()

                @pl.when((c <= o) & has_r)
                def _():
                    if not far:
                        a_copy(c, p, a_rs, to_r).start()
                    b_copy(t, p, b_rs.at[t, p], to_r).start()

                @pl.when((c >= o) & has_l)
                def _():
                    if not far:
                        a_copy(c, p, a_ls, to_l).start()
                    b_copy(t, p, b_ls.at[t, p], to_l).start()

    def multiply(s):
        @pl.loop(0, 2 * n)
        def _(k):
            far = (k >= n).astype(jnp.int32)
            c = k - far * n
            p = s - (n - 1) - jnp.abs(o - c) - far
            t = jnp.where(far > 0, other, i) * n + c

            @pl.when(inside(p))
            def _():
                at = pl.multiple_of(t * local + p * cols, cols)
                value = jnp.concatenate([ga[t, p], gb[t, p]], axis=1).astype(F32)
                square = value * value
                part = square[:, :128]
                for j in range(1, cols // 128):
                    part += square[:, j * 128:(j + 1) * 128]
                sq[...] += part
                scaled = (value * gains[:, pl.ds(at, cols)]).astype(BF16)
                acc[...] += jnp.dot(
                    scaled, w[pl.ds(at, cols), :], preferred_element_type=F32
                )

    @pl.loop(0, pieces + 2 * n - 1)
    def _(s):
        send_y(s + AHEAD)
        passing(s)
        finish(s)
        spread(s, 0)
        spread(s, 1)

        @pl.when(s == n - 1)
        def _():
            loads[3].wait()

        multiply(s)

    factor = lax.rsqrt(jnp.sum(sq[...], axis=1, keepdims=True) / width + 1e-05)
    kv_out[...] = (acc[...] * factor).astype(BF16)

    @pl.loop(0, pieces)
    def _(p):
        me = i * n + o
        b_copy(me, p, b_ys.at[p], to_y).wait_send()
        for d in range(n):
            y_copy(d, p).wait_send()
            a_copy(d, p, a_ys, to_y).wait_send()

            @pl.when(d > o)
            def _():
                r_copy(d, p).wait_send()

            @pl.when(d < o)
            def _():
                l_copy(d, p).wait_send()

            @pl.when((d <= o) & has_r)
            def _():
                a_copy(d, p, a_rs, to_r).wait_send()
                for t in (d, n + d):
                    b_copy(t, p, b_rs.at[t, p], to_r).wait_send()

            @pl.when((d >= o) & has_l)
            def _():
                a_copy(d, p, a_ls, to_l).wait_send()
                for t in (d, n + d):
                    b_copy(t, p, b_ls.at[t, p], to_l).wait_send()


def body(n, partials, residual, norm_gain, kv_weight):
    rows, local = residual.shape
    width = norm_gain.shape[0]
    heads_local, pair = kv_weight.shape[1:]
    pieces = PIECES
    cols = local // pieces
    wide = heads_local * pair
    dma = pltpu.SemaphoreType.DMA
    vmem = pltpu.VMEM
    stream, kv = pl.pallas_call(
        functools.partial(fused, n, pieces),
        out_shape=(
            jax.ShapeDtypeStruct((rows, local), BF16),
            jax.ShapeDtypeStruct((rows, wide), BF16),
        ),
        in_specs=[pl.BlockSpec(memory_space=pl.ANY)] * 4,
        out_specs=(pl.BlockSpec(memory_space=pltpu.VMEM),) * 2,
        scratch_shapes=[
            vmem((rows, n * local), BF16),
            vmem((rows, local), BF16),
            vmem((1, width), F32),
            vmem((width, wide), BF16),
            vmem((n, pieces, rows, cols), BF16),
            vmem((n, pieces, rows, cols), BF16),
            vmem((n, pieces, rows, cols), BF16),
            vmem((2 * n, pieces, rows, cols // 2), BF16),
            vmem((2 * n, pieces, rows, cols // 2), BF16),
            vmem((rows, cols), F32),
            vmem((rows, wide), F32),
            vmem((rows, 128), F32),
            dma((4,)),
            dma((n, pieces)), dma((n, pieces)),
            dma((n, pieces)), dma((n, pieces)),
            dma((n, pieces)), dma((n, pieces)),
            dma((2 * n, pieces)),
            dma((n, pieces)), dma((n, pieces)), dma((n, pieces)),
            dma((2 * n, pieces)),
            dma((2 * n, pieces)), dma((2 * n, pieces)), dma((pieces,)),
        ],
        compiler_params=pltpu.CompilerParams(
            collective_id=0, has_side_effects=True, vmem_limit_bytes=60 * 1024 * 1024
        ),
        cost_estimate=pl.CostEstimate(
            flops=2 * rows * width * wide,
            bytes_accessed=2 * (rows * width + width * wide),
            transcendentals=rows,
        ),
    )(partials, residual, norm_gain.reshape(1, width), kv_weight.reshape(width, wide))
    return stream, kv.reshape(rows, heads_local, pair)


def solution(mesh):
    placed = (
        P(("dp", "inner", "outer"), None, None),
        P("dp", ("inner", "outer")),
        P(),
        P(None, ("inner", "outer"), None),
    )
    return jax.shard_map(
        functools.partial(body, mesh.shape["outer"]),
        mesh=mesh,
        in_specs=placed,
        out_specs=(P("dp", ("inner", "outer")), P("dp", ("inner", "outer"), None)),
        check_vma=False,
    )
```

```python
import functools

import jax
import jax.numpy as jnp
from jax import lax
from jax.experimental import pallas as pl
from jax.experimental.pallas import tpu as pltpu
from jax.sharding import PartitionSpec as P

MESH = pl.DeviceIdType.MESH
F32 = jnp.float32
BF16 = jnp.bfloat16
PIECES = 8
AHEAD = 11


def fused(n, pieces, partials, residual, gain, weight, stream_out, kv_out,
          mine, resid, gains, w, ybuf, rbuf, lbuf, ga, gb, tmp, acc, sq,
          loc, y_s, y_r, r_s, r_r, l_s, l_r, a_r, a_rs, a_ls, a_ys,
          b_r, b_rs, b_ls, b_ys):
    i = lax.axis_index("inner")
    o = lax.axis_index("outer")
    other = 1 - i
    rows, local = resid.shape
    width = gains.shape[1]
    half = n * local
    cols = local // pieces
    cut = cols // 2
    to_y = {"inner": other}
    to_r = {"outer": jnp.minimum(o + 1, n - 1)}
    to_l = {"outer": jnp.maximum(o - 1, 0)}
    has_r = o < n - 1
    has_l = o > 0

    loads = [
        pltpu.make_async_copy(
            partials.at[0, :, pl.ds(pl.multiple_of(i * half, half), half)], mine, loc.at[0]
        ),
        pltpu.make_async_copy(residual, resid, loc.at[1]),
        pltpu.make_async_copy(gain, gains, loc.at[2]),
        pltpu.make_async_copy(weight, w, loc.at[3]),
    ]

    def remote(src, dst, ssem, rsem, to):
        return pltpu.make_async_remote_copy(
            src_ref=src, dst_ref=dst, send_sem=ssem, recv_sem=rsem,
            device_id=to, device_id_type=MESH,
        )

    def y_copy(d, p):
        at = pl.multiple_of(other * half + d * local + p * cols, cols)
        return remote(partials.at[0, :, pl.ds(at, cols)], ybuf.at[d, p],
                      y_s.at[d, p], y_r.at[d, p], to_y)

    def r_copy(d, p):
        return remote(rbuf.at[d, p], rbuf.at[d, p], r_s.at[d, p], r_r.at[d, p], to_r)

    def l_copy(d, p):
        return remote(lbuf.at[d, p], lbuf.at[d, p], l_s.at[d, p], l_r.at[d, p], to_l)

    def a_copy(c, p, ssem, to):
        t = i * n + c
        return remote(ga.at[t, p], ga.at[t, p], ssem.at[c, p], a_r.at[t, p], to)

    def b_copy(t, p, ssem, to):
        return remote(gb.at[t, p], gb.at[t, p], ssem, b_r.at[t, p], to)

    def inside(p):
        return (p >= 0) & (p < pieces)

    def level_one(d, p):
        y_copy(d, p).wait_recv()
        at = pl.multiple_of(d * local + p * cols, cols)
        return mine[:, pl.ds(at, cols)].astype(F32) + ybuf[d, p].astype(F32)

    def skew(d):
        return jnp.where(d > o, o, jnp.where(d < o, n - 1 - o, n - 1))

    def send_y(s):
        for d in range(n):
            p = s - skew(d)

            @pl.when(inside(p))
            def _():
                y_copy(d, p).start()

    barrier = pltpu.get_barrier_semaphore()
    pl.semaphore_signal(barrier, inc=1, device_id=to_y, device_id_type=MESH)

    @pl.when(has_r)
    def _():
        pl.semaphore_signal(barrier, inc=1, device_id=to_r, device_id_type=MESH)

    @pl.when(has_l)
    def _():
        pl.semaphore_signal(barrier, inc=1, device_id=to_l, device_id_type=MESH)

    pl.semaphore_wait(barrier, 1 + has_r.astype(jnp.int32) + has_l.astype(jnp.int32))
    for s in range(AHEAD):
        send_y(jnp.int32(s))
    for load in loads:
        load.start()
    acc[...] = jnp.zeros_like(acc)
    sq[...] = jnp.zeros_like(sq)
    for load in loads[:3]:
        load.wait()

    def passing(s):
        p = s - o

        @pl.when(inside(p) & has_r)
        def _():
            for d in reversed(range(n)):
                @pl.when(d > o)
                def _():
                    value = level_one(d, p)

                    @pl.when(has_l)
                    def _():
                        r_copy(d, p).wait_recv()
                        rbuf[d, p] = (value + rbuf[d, p].astype(F32)).astype(BF16)

                    @pl.when(jnp.logical_not(has_l))
                    def _():
                        rbuf[d, p] = value.astype(BF16)

                    r_copy(d, p).start()

        q = s - (n - 1 - o)

        @pl.when(inside(q) & has_l)
        def _():
            for d in range(n):
                @pl.when(d < o)
                def _():
                    value = level_one(d, q)

                    @pl.when(has_r)
                    def _():
                        l_copy(d, q).wait_recv()
                        lbuf[d, q] = (value + lbuf[d, q].astype(F32)).astype(BF16)

                    @pl.when(jnp.logical_not(has_r))
                    def _():
                        lbuf[d, q] = value.astype(BF16)

                    l_copy(d, q).start()

    def finish(s):
        p = s - (n - 1)

        @pl.when(inside(p))
        def _():
            at = pl.multiple_of(p * cols, cols)
            tmp[...] = level_one(o, p) + resid[:, pl.ds(at, cols)].astype(F32)

            @pl.when(has_l)
            def _():
                r_copy(o, p).wait_recv()
                tmp[...] += rbuf[o, p].astype(F32)

            @pl.when(has_r)
            def _():
                l_copy(o, p).wait_recv()
                tmp[...] += lbuf[o, p].astype(F32)

            value = tmp[...].astype(BF16)
            stream_out[:, pl.ds(at, cols)] = value
            me = i * n + o
            ga[me, p] = value[:, :cut]
            gb[me, p] = value[:, cut:]
            b_copy(me, p, b_ys.at[p], to_y).start()

    def spread(s, far):
        for c in range(n):
            p = s - (n - 1) - jnp.abs(o - c) - far
            t = (other if far else i) * n + c

            @pl.when(inside(p))
            def _():
                if far:
                    a_in = remote(ga.at[t, p], ga.at[t, p], a_ys.at[c, p], a_r.at[t, p], to_y)
                    a_in.wait_recv()
                    b_copy(t, p, b_ys.at[p], to_y).wait_recv()
                else:
                    @pl.when(c != o)
                    def _():
                        a_copy(c, p, a_ys, to_y).wait_recv()
                        b_copy(t, p, b_ys.at[p], to_y).wait_recv()
                    a_copy(c, p, a_ys, to_y).start()

                @pl.when((c <= o) & has_r)
                def _():
                    if not far:
                        a_copy(c, p, a_rs, to_r).start()
                    b_copy(t, p, b_rs.at[t, p], to_r).start()

                @pl.when((c >= o) & has_l)
                def _():
                    if not far:
                        a_copy(c, p, a_ls, to_l).start()
                    b_copy(t, p, b_ls.at[t, p], to_l).start()

    def multiply(s):
        @pl.loop(0, 2 * n)
        def _(k):
            far = (k >= n).astype(jnp.int32)
            c = k - far * n
            p = s - (n - 1) - jnp.abs(o - c) - far
            t = jnp.where(far > 0, other, i) * n + c

            @pl.when(inside(p))
            def _():
                at = pl.multiple_of(t * local + p * cols, cols)
                value = jnp.concatenate([ga[t, p], gb[t, p]], axis=1).astype(F32)
                square = value * value
                part = square[:, :128]
                for j in range(1, cols // 128):
                    part += square[:, j * 128:(j + 1) * 128]
                sq[...] += part
                scaled = (value * gains[:, pl.ds(at, cols)]).astype(BF16)
                acc[...] += jnp.dot(
                    scaled, w[pl.ds(at, cols), :], preferred_element_type=F32
                )

    @pl.loop(0, pieces + 2 * n - 1)
    def _(s):
        send_y(s + AHEAD)
        passing(s)
        finish(s)
        spread(s, 0)
        spread(s, 1)

        @pl.when(s == n - 1)
        def _():
            loads[3].wait()

        multiply(s)

    factor = lax.rsqrt(jnp.sum(sq[...], axis=1, keepdims=True) / width + 1e-05)
    kv_out[...] = (acc[...] * factor).astype(BF16)

    @pl.loop(0, pieces)
    def _(p):
        me = i * n + o
        b_copy(me, p, b_ys.at[p], to_y).wait_send()
        for d in range(n):
            y_copy(d, p).wait_send()
            a_copy(d, p, a_ys, to_y).wait_send()

            @pl.when(d > o)
            def _():
                r_copy(d, p).wait_send()

            @pl.when(d < o)
            def _():
                l_copy(d, p).wait_send()

            @pl.when((d <= o) & has_r)
            def _():
                a_copy(d, p, a_rs, to_r).wait_send()
                for t in (d, n + d):
                    b_copy(t, p, b_rs.at[t, p], to_r).wait_send()

            @pl.when((d >= o) & has_l)
            def _():
                a_copy(d, p, a_ls, to_l).wait_send()
                for t in (d, n + d):
                    b_copy(t, p, b_ls.at[t, p], to_l).wait_send()


def body(n, partials, residual, norm_gain, kv_weight):
    rows, local = residual.shape
    width = norm_gain.shape[0]
    heads_local, pair = kv_weight.shape[1:]
    pieces = PIECES
    cols = local // pieces
    wide = heads_local * pair
    dma = pltpu.SemaphoreType.DMA
    vmem = pltpu.VMEM
    stream, kv = pl.pallas_call(
        functools.partial(fused, n, pieces),
        out_shape=(
            jax.ShapeDtypeStruct((rows, local), BF16),
            jax.ShapeDtypeStruct((rows, wide), BF16),
        ),
        in_specs=[pl.BlockSpec(memory_space=pl.ANY)] * 4,
        out_specs=(pl.BlockSpec(memory_space=pltpu.VMEM),) * 2,
        scratch_shapes=[
            vmem((rows, n * local), BF16),
            vmem((rows, local), BF16),
            vmem((1, width), F32),
            vmem((width, wide), BF16),
            vmem((n, pieces, rows, cols), BF16),
            vmem((n, pieces, rows, cols), BF16),
            vmem((n, pieces, rows, cols), BF16),
            vmem((2 * n, pieces, rows, cols // 2), BF16),
            vmem((2 * n, pieces, rows, cols // 2), BF16),
            vmem((rows, cols), F32),
            vmem((rows, wide), F32),
            vmem((rows, 128), F32),
            dma((4,)),
            dma((n, pieces)), dma((n, pieces)),
            dma((n, pieces)), dma((n, pieces)),
            dma((n, pieces)), dma((n, pieces)),
            dma((2 * n, pieces)),
            dma((n, pieces)), dma((n, pieces)), dma((n, pieces)),
            dma((2 * n, pieces)),
            dma((2 * n, pieces)), dma((2 * n, pieces)), dma((pieces,)),
        ],
        compiler_params=pltpu.CompilerParams(
            collective_id=0, has_side_effects=True, vmem_limit_bytes=60 * 1024 * 1024
        ),
        cost_estimate=pl.CostEstimate(
            flops=2 * rows * width * wide,
            bytes_accessed=2 * (rows * width + width * wide),
            transcendentals=rows,
        ),
    )(partials, residual, norm_gain.reshape(1, width), kv_weight.reshape(width, wide))
    return stream, kv.reshape(rows, heads_local, pair)


def solution(mesh):
    placed = (
        P(("dp", "inner", "outer"), None, None),
        P("dp", ("inner", "outer")),
        P(),
        P(None, ("inner", "outer"), None),
    )
    return jax.shard_map(
        functools.partial(body, mesh.shape["outer"]),
        mesh=mesh,
        in_specs=placed,
        out_specs=(P("dp", ("inner", "outer")), P("dp", ("inner", "outer"), None)),
        check_vma=False,
    )
```

```python
import functools

import jax
import jax.numpy as jnp
from jax import lax
from jax.experimental import pallas as pl
from jax.experimental.pallas import tpu as pltpu
from jax.sharding import PartitionSpec as P

MESH = pl.DeviceIdType.MESH
F32 = jnp.float32
BF16 = jnp.bfloat16
PIECES = 8
AHEAD = 2


def fused(n, pieces, partials, residual, gain, weight, stream_out, kv_out,
          mine, resid, gains, w, ybuf, rbuf, lbuf, ga, gb, tmp, acc, sq,
          loc, y_s, y_r, r_s, r_r, l_s, l_r, a_r, a_rs, a_ls, a_ys,
          b_r, b_rs, b_ls, b_ys):
    i = lax.axis_index("inner")
    o = lax.axis_index("outer")
    other = 1 - i
    rows, local = resid.shape
    width = gains.shape[1]
    half = n * local
    cols = local // pieces
    cut = cols // 2
    to_y = {"inner": other}
    to_r = {"outer": jnp.minimum(o + 1, n - 1)}
    to_l = {"outer": jnp.maximum(o - 1, 0)}
    has_r = o < n - 1
    has_l = o > 0

    loads = [
        pltpu.make_async_copy(
            partials.at[0, :, pl.ds(pl.multiple_of(i * half, half), half)], mine, loc.at[0]
        ),
        pltpu.make_async_copy(residual, resid, loc.at[1]),
        pltpu.make_async_copy(gain, gains, loc.at[2]),
        pltpu.make_async_copy(weight, w, loc.at[3]),
    ]

    def remote(src, dst, ssem, rsem, to):
        return pltpu.make_async_remote_copy(
            src_ref=src, dst_ref=dst, send_sem=ssem, recv_sem=rsem,
            device_id=to, device_id_type=MESH,
        )

    def y_copy(d, p):
        at = pl.multiple_of(other * half + d * local + p * cols, cols)
        return remote(partials.at[0, :, pl.ds(at, cols)], ybuf.at[d, p],
                      y_s.at[d, p], y_r.at[d, p], to_y)

    def r_copy(d, p):
        return remote(rbuf.at[d, p], rbuf.at[d, p], r_s.at[d, p], r_r.at[d, p], to_r)

    def l_copy(d, p):
        return remote(lbuf.at[d, p], lbuf.at[d, p], l_s.at[d, p], l_r.at[d, p], to_l)

    def a_copy(c, p, ssem, to):
        t = i * n + c
        return remote(ga.at[t, p], ga.at[t, p], ssem.at[c, p], a_r.at[t, p], to)

    def b_copy(t, p, ssem, to):
        return remote(gb.at[t, p], gb.at[t, p], ssem, b_r.at[t, p], to)

    def inside(p):
        return (p >= 0) & (p < pieces)

    def level_one(d, p):
        y_copy(d, p).wait_recv()
        at = pl.multiple_of(d * local + p * cols, cols)
        return mine[:, pl.ds(at, cols)].astype(F32) + ybuf[d, p].astype(F32)

    def skew(d):
        return jnp.where(d > o, o, jnp.where(d < o, n - 1 - o, n - 1))

    def send_y(s):
        for d in range(n):
            p = s - skew(d)

            @pl.when(inside(p))
            def _():
                y_copy(d, p).start()

    barrier = pltpu.get_barrier_semaphore()
    pl.semaphore_signal(barrier, inc=1, device_id=to_y, device_id_type=MESH)

    @pl.when(has_r)
    def _():
        pl.semaphore_signal(barrier, inc=1, device_id=to_r, device_id_type=MESH)

    @pl.when(has_l)
    def _():
        pl.semaphore_signal(barrier, inc=1, device_id=to_l, device_id_type=MESH)

    pl.semaphore_wait(barrier, 1 + has_r.astype(jnp.int32) + has_l.astype(jnp.int32))
    for s in range(AHEAD):
        send_y(jnp.int32(s))
    for load in loads:
        load.start()
    acc[...] = jnp.zeros_like(acc)
    sq[...] = jnp.zeros_like(sq)
    for load in loads[:3]:
        load.wait()

    def passing(s):
        p = s - o

        @pl.when(inside(p) & has_r)
        def _():
            for d in reversed(range(n)):
                @pl.when(d > o)
                def _():
                    value = level_one(d, p)

                    @pl.when(has_l)
                    def _():
                        r_copy(d, p).wait_recv()
                        rbuf[d, p] = (value + rbuf[d, p].astype(F32)).astype(BF16)

                    @pl.when(jnp.logical_not(has_l))
                    def _():
                        rbuf[d, p] = value.astype(BF16)

                    r_copy(d, p).start()

        q = s - (n - 1 - o)

        @pl.when(inside(q) & has_l)
        def _():
            for d in range(n):
                @pl.when(d < o)
                def _():
                    value = level_one(d, q)

                    @pl.when(has_r)
                    def _():
                        l_copy(d, q).wait_recv()
                        lbuf[d, q] = (value + lbuf[d, q].astype(F32)).astype(BF16)

                    @pl.when(jnp.logical_not(has_r))
                    def _():
                        lbuf[d, q] = value.astype(BF16)

                    l_copy(d, q).start()

    def finish(s):
        p = s - (n - 1)

        @pl.when(inside(p))
        def _():
            at = pl.multiple_of(p * cols, cols)
            tmp[...] = level_one(o, p) + resid[:, pl.ds(at, cols)].astype(F32)

            @pl.when(has_l)
            def _():
                r_copy(o, p).wait_recv()
                tmp[...] += rbuf[o, p].astype(F32)

            @pl.when(has_r)
            def _():
                l_copy(o, p).wait_recv()
                tmp[...] += lbuf[o, p].astype(F32)

            value = tmp[...].astype(BF16)
            stream_out[:, pl.ds(at, cols)] = value
            me = i * n + o
            ga[me, p] = value[:, :cut]
            gb[me, p] = value[:, cut:]
            b_copy(me, p, b_ys.at[p], to_y).start()

    def spread(s, far):
        for c in range(n):
            p = s - (n - 1) - jnp.abs(o - c) - far
            t = (other if far else i) * n + c

            @pl.when(inside(p))
            def _():
                if far:
                    a_in = remote(ga.at[t, p], ga.at[t, p], a_ys.at[c, p], a_r.at[t, p], to_y)
                    a_in.wait_recv()
                    b_copy(t, p, b_ys.at[p], to_y).wait_recv()
                else:
                    @pl.when(c != o)
                    def _():
                        a_copy(c, p, a_ys, to_y).wait_recv()
                        b_copy(t, p, b_ys.at[p], to_y).wait_recv()
                    a_copy(c, p, a_ys, to_y).start()

                @pl.when((c <= o) & has_r)
                def _():
                    if not far:
                        a_copy(c, p, a_rs, to_r).start()
                    b_copy(t, p, b_rs.at[t, p], to_r).start()

                @pl.when((c >= o) & has_l)
                def _():
                    if not far:
                        a_copy(c, p, a_ls, to_l).start()
                    b_copy(t, p, b_ls.at[t, p], to_l).start()

    def multiply(s):
        @pl.loop(0, 2 * n)
        def _(k):
            far = (k >= n).astype(jnp.int32)
            c = k - far * n
            p = s - (n - 1) - jnp.abs(o - c) - far
            t = jnp.where(far > 0, other, i) * n + c

            @pl.when(inside(p))
            def _():
                at = pl.multiple_of(t * local + p * cols, cols)
                value = jnp.concatenate([ga[t, p], gb[t, p]], axis=1).astype(F32)
                square = value * value
                part = square[:, :128]
                for j in range(1, cols // 128):
                    part += square[:, j * 128:(j + 1) * 128]
                sq[...] += part
                scaled = (value * gains[:, pl.ds(at, cols)]).astype(BF16)
                acc[...] += jnp.dot(
                    scaled, w[pl.ds(at, cols), :], preferred_element_type=F32
                )

    @pl.loop(0, pieces + 2 * n - 1)
    def _(s):
        passing(s)
        finish(s)
        spread(s, 0)
        spread(s, 1)
        send_y(s + AHEAD)

        @pl.when(s == n - 1)
        def _():
            loads[3].wait()

        multiply(s)

    factor = lax.rsqrt(jnp.sum(sq[...], axis=1, keepdims=True) / width + 1e-05)
    kv_out[...] = (acc[...] * factor).astype(BF16)

    @pl.loop(0, pieces)
    def _(p):
        me = i * n + o
        b_copy(me, p, b_ys.at[p], to_y).wait_send()
        for d in range(n):
            y_copy(d, p).wait_send()
            a_copy(d, p, a_ys, to_y).wait_send()

            @pl.when(d > o)
            def _():
                r_copy(d, p).wait_send()

            @pl.when(d < o)
            def _():
                l_copy(d, p).wait_send()

            @pl.when((d <= o) & has_r)
            def _():
                a_copy(d, p, a_rs, to_r).wait_send()
                for t in (d, n + d):
                    b_copy(t, p, b_rs.at[t, p], to_r).wait_send()

            @pl.when((d >= o) & has_l)
            def _():
                a_copy(d, p, a_ls, to_l).wait_send()
                for t in (d, n + d):
                    b_copy(t, p, b_ls.at[t, p], to_l).wait_send()


def body(n, partials, residual, norm_gain, kv_weight):
    rows, local = residual.shape
    width = norm_gain.shape[0]
    heads_local, pair = kv_weight.shape[1:]
    pieces = PIECES
    cols = local // pieces
    wide = heads_local * pair
    dma = pltpu.SemaphoreType.DMA
    vmem = pltpu.VMEM
    stream, kv = pl.pallas_call(
        functools.partial(fused, n, pieces),
        out_shape=(
            jax.ShapeDtypeStruct((rows, local), BF16),
            jax.ShapeDtypeStruct((rows, wide), BF16),
        ),
        in_specs=[pl.BlockSpec(memory_space=pl.ANY)] * 4,
        out_specs=(pl.BlockSpec(memory_space=pltpu.VMEM),) * 2,
        scratch_shapes=[
            vmem((rows, n * local), BF16),
            vmem((rows, local), BF16),
            vmem((1, width), F32),
            vmem((width, wide), BF16),
            vmem((n, pieces, rows, cols), BF16),
            vmem((n, pieces, rows, cols), BF16),
            vmem((n, pieces, rows, cols), BF16),
            vmem((2 * n, pieces, rows, cols // 2), BF16),
            vmem((2 * n, pieces, rows, cols // 2), BF16),
            vmem((rows, cols), F32),
            vmem((rows, wide), F32),
            vmem((rows, 128), F32),
            dma((4,)),
            dma((n, pieces)), dma((n, pieces)),
            dma((n, pieces)), dma((n, pieces)),
            dma((n, pieces)), dma((n, pieces)),
            dma((2 * n, pieces)),
            dma((n, pieces)), dma((n, pieces)), dma((n, pieces)),
            dma((2 * n, pieces)),
            dma((2 * n, pieces)), dma((2 * n, pieces)), dma((pieces,)),
        ],
        compiler_params=pltpu.CompilerParams(
            collective_id=0, has_side_effects=True, vmem_limit_bytes=60 * 1024 * 1024
        ),
        cost_estimate=pl.CostEstimate(
            flops=2 * rows * width * wide,
            bytes_accessed=2 * (rows * width + width * wide),
            transcendentals=rows,
        ),
    )(partials, residual, norm_gain.reshape(1, width), kv_weight.reshape(width, wide))
    return stream, kv.reshape(rows, heads_local, pair)


def solution(mesh):
    placed = (
        P(("dp", "inner", "outer"), None, None),
        P("dp", ("inner", "outer")),
        P(),
        P(None, ("inner", "outer"), None),
    )
    return jax.shard_map(
        functools.partial(body, mesh.shape["outer"]),
        mesh=mesh,
        in_specs=placed,
        out_specs=(P("dp", ("inner", "outer")), P("dp", ("inner", "outer"), None)),
        check_vma=False,
    )
```

```python
import functools

import jax
import jax.numpy as jnp
from jax import lax
from jax.experimental import pallas as pl
from jax.experimental.pallas import tpu as pltpu
from jax.sharding import PartitionSpec as P

MESH = pl.DeviceIdType.MESH
F32 = jnp.float32
BF16 = jnp.bfloat16
PIECES = 16
AHEAD = 3
CYCLE = 2
EARLY = 1


def fused(n, pieces, partials, residual, gain, weight, stream_out, kv_out,
          mine, resid, gains, w, ybuf, rbuf, lbuf, g, tmp, acc, sq,
          loc, out_s, y_r, r_r, l_r, g_r):
    i = lax.axis_index("inner")
    o = lax.axis_index("outer")
    other = 1 - i
    rows, local = resid.shape
    width = gains.shape[1]
    half = n * local
    cols = local // pieces
    group = max(1, 256 // cols)
    early = sum(p % CYCLE < EARLY for p in range(pieces))
    to_y = {"inner": other}
    to_r = {"outer": jnp.minimum(o + 1, n - 1)}
    to_l = {"outer": jnp.maximum(o - 1, 0)}
    has_r = o < n - 1
    has_l = o > 0

    loads = [
        pltpu.make_async_copy(
            partials.at[0, :, pl.ds(pl.multiple_of(i * half, half), half)], mine, loc.at[0]
        ),
        pltpu.make_async_copy(residual, resid, loc.at[1]),
        pltpu.make_async_copy(gain, gains, loc.at[2]),
        pltpu.make_async_copy(weight, w, loc.at[3]),
    ]

    def remote(src, dst, ssem, rsem, to):
        return pltpu.make_async_remote_copy(
            src_ref=src, dst_ref=dst, send_sem=ssem, recv_sem=rsem,
            device_id=to, device_id_type=MESH,
        )

    def y_copy(d, p):
        at = pl.multiple_of(other * half + d * local + p * cols, cols)
        return remote(partials.at[0, :, pl.ds(at, cols)], ybuf.at[d, p],
                      out_s.at[0], y_r.at[d, p], to_y)

    def r_copy(d, p):
        return remote(rbuf.at[d, p], rbuf.at[d, p], out_s.at[1], r_r.at[d, p], to_r)

    def l_copy(d, p):
        return remote(lbuf.at[d, p], lbuf.at[d, p], out_s.at[1], l_r.at[d, p], to_l)

    def g_copy(t, p, kind, to):
        k = t * pieces + p
        return remote(g.at[k], g.at[k], out_s.at[kind], g_r.at[k], to)

    def inside(p):
        return (p >= 0) & (p < pieces)

    def is_early(p):
        return lax.rem(p, CYCLE) < EARLY

    def level_one(d, p):
        y_copy(d, p).wait_recv()
        at = pl.multiple_of(d * local + p * cols, cols)
        return mine[:, pl.ds(at, cols)].astype(F32) + ybuf[d, p].astype(F32)

    def skew(d):
        return jnp.where(d > o, o, jnp.where(d < o, n - 1 - o, n - 1))

    def send_y(s):
        for d in range(n):
            p = s - skew(d)

            @pl.when(inside(p))
            def _():
                y_copy(d, p).start()

    barrier = pltpu.get_barrier_semaphore()
    pl.semaphore_signal(barrier, inc=1, device_id=to_y, device_id_type=MESH)

    @pl.when(has_r)
    def _():
        pl.semaphore_signal(barrier, inc=1, device_id=to_r, device_id_type=MESH)

    @pl.when(has_l)
    def _():
        pl.semaphore_signal(barrier, inc=1, device_id=to_l, device_id_type=MESH)

    for load in loads[:3]:
        load.start()
    pl.semaphore_wait(barrier, 1 + has_r.astype(jnp.int32) + has_l.astype(jnp.int32))
    for s in range(AHEAD):
        send_y(jnp.int32(s))
    loads[3].start()
    acc[...] = jnp.zeros_like(acc)
    sq[...] = jnp.zeros_like(sq)
    for load in loads[:3]:
        load.wait()

    def passing(s):
        p = s - o

        @pl.when(inside(p) & has_r)
        def _():
            for d in reversed(range(n)):
                @pl.when(d > o)
                def _():
                    value = level_one(d, p)

                    @pl.when(has_l)
                    def _():
                        r_copy(d, p).wait_recv()
                        rbuf[d, p] = (value + rbuf[d, p].astype(F32)).astype(BF16)

                    @pl.when(jnp.logical_not(has_l))
                    def _():
                        rbuf[d, p] = value.astype(BF16)

                    r_copy(d, p).start()

        q = s - (n - 1 - o)

        @pl.when(inside(q) & has_l)
        def _():
            for d in range(n):
                @pl.when(d < o)
                def _():
                    value = level_one(d, q)

                    @pl.when(has_r)
                    def _():
                        l_copy(d, q).wait_recv()
                        lbuf[d, q] = (value + lbuf[d, q].astype(F32)).astype(BF16)

                    @pl.when(jnp.logical_not(has_r))
                    def _():
                        lbuf[d, q] = value.astype(BF16)

                    l_copy(d, q).start()

    def finish(s):
        p = s - (n - 1)

        @pl.when(inside(p))
        def _():
            at = pl.multiple_of(p * cols, cols)
            tmp[...] = level_one(o, p) + resid[:, pl.ds(at, cols)].astype(F32)

            @pl.when(has_l)
            def _():
                r_copy(o, p).wait_recv()
                tmp[...] += rbuf[o, p].astype(F32)

            @pl.when(has_r)
            def _():
                l_copy(o, p).wait_recv()
                tmp[...] += lbuf[o, p].astype(F32)

            value = tmp[...].astype(BF16)
            stream_out[:, pl.ds(at, cols)] = value
            me = i * n + o
            g[me * pieces + p] = value

            @pl.when(is_early(p))
            def _():
                g_copy(me, p, 2, to_y).start()

    def along(c, t, p, kind):
        @pl.when((c <= o) & has_r)
        def _():
            g_copy(t, p, kind, to_r).start()

        @pl.when((c >= o) & has_l)
        def _():
            g_copy(t, p, kind, to_l).start()

    def near(s):
        for c in range(n):
            p = s - (n - 1) - jnp.abs(o - c)
            t = i * n + c

            @pl.when(inside(p))
            def _():
                @pl.when(c != o)
                def _():
                    g_copy(t, p, 3, to_r).wait_recv()

                along(c, t, p, 3)

                @pl.when(jnp.logical_not(is_early(p)))
                def _():
                    g_copy(t, p, 2, to_y).start()

    def far(s):
        for c in range(n):
            p = s - n - jnp.abs(o - c)
            t = other * n + c

            @pl.when(inside(p))
            def _():
                g_copy(t, p, 2, to_y).wait_recv()

                @pl.when(is_early(p))
                def _():
                    along(c, t, p, 4)

    def multiply(s):
        @pl.loop(0, 2 * n)
        def _(k):
            away = (k >= n).astype(jnp.int32)
            c = k - away * n
            p = s - (n - 1) - jnp.abs(o - c) - away
            t = jnp.where(away > 0, other, i) * n + c

            @pl.when(inside(p) & (lax.rem(p, group) == group - 1))
            def _():
                first = p - (group - 1)
                at = pl.multiple_of(t * local + first * cols, group * cols)
                parts = [g[t * pieces + first + j] for j in range(group)]
                value = jnp.concatenate(parts, axis=1).astype(F32)
                square = value * value
                part = square[:, :128]
                for j in range(1, group * cols // 128):
                    part += square[:, j * 128:(j + 1) * 128]
                sq[...] += part
                scaled = (value * gains[:, pl.ds(at, group * cols)]).astype(BF16)
                acc[...] += jnp.dot(
                    scaled, w[pl.ds(at, group * cols), :], preferred_element_type=F32
                )

    @pl.loop(0, pieces + 2 * n - 1)
    def _(s):
        send_y(s + AHEAD)
        passing(s)
        finish(s)
        near(s)
        far(s)

        @pl.when(s == n - 1)
        def _():
            loads[3].wait()

        multiply(s)

    factor = lax.rsqrt(jnp.sum(sq[...], axis=1, keepdims=True) / width + 1e-05)
    kv_out[...] = (acc[...] * factor).astype(BF16)

    def sent(ref, kind):
        remote(ref, ref, out_s.at[kind], g_r.at[0], to_y).wait_send()

    sent(ybuf, 0)
    sent(rbuf.at[pl.ds(0, n - 1)], 1)
    sent(g.at[pl.ds(0, n * (pieces - early) + early)], 2)

    @pl.when(has_l & has_r)
    def _():
        sent(g.at[pl.ds(0, (n + 1) * pieces)], 3)
        sent(g.at[pl.ds(0, (n + 1) * early)], 4)

    @pl.when(jnp.logical_not(has_l & has_r))
    def _():
        sent(g.at[pl.ds(0, pieces)], 3)
        sent(g.at[pl.ds(0, early)], 4)


def body(n, partials, residual, norm_gain, kv_weight):
    rows, local = residual.shape
    width = norm_gain.shape[0]
    heads_local, pair = kv_weight.shape[1:]
    pieces = PIECES
    cols = local // pieces
    wide = heads_local * pair
    dma = pltpu.SemaphoreType.DMA
    vmem = pltpu.VMEM
    stream, kv = pl.pallas_call(
        functools.partial(fused, n, pieces),
        out_shape=(
            jax.ShapeDtypeStruct((rows, local), BF16),
            jax.ShapeDtypeStruct((rows, wide), BF16),
        ),
        in_specs=[pl.BlockSpec(memory_space=pl.ANY)] * 4,
        out_specs=(pl.BlockSpec(memory_space=pltpu.VMEM),) * 2,
        scratch_shapes=[
            vmem((rows, n * local), BF16),
            vmem((rows, local), BF16),
            vmem((1, width), F32),
            vmem((width, wide), BF16),
            vmem((n, pieces, rows, cols), BF16),
            vmem((n, pieces, rows, cols), BF16),
            vmem((n, pieces, rows, cols), BF16),
            vmem((2 * n * pieces, rows, cols), BF16),
            vmem((rows, cols), F32),
            vmem((rows, wide), F32),
            vmem((rows, 128), F32),
            dma((4,)),
            dma((5,)),
            dma((n, pieces)),
            dma((n, pieces)),
            dma((n, pieces)),
            dma((2 * n * pieces,)),
        ],
        compiler_params=pltpu.CompilerParams(
            collective_id=0, has_side_effects=True, vmem_limit_bytes=60 * 1024 * 1024
        ),
        cost_estimate=pl.CostEstimate(
            flops=2 * rows * width * wide,
            bytes_accessed=2 * (rows * width + width * wide),
            transcendentals=rows,
        ),
    )(partials, residual, norm_gain.reshape(1, width), kv_weight.reshape(width, wide))
    return stream, kv.reshape(rows, heads_local, pair)


def solution(mesh):
    placed = (
        P(("dp", "inner", "outer"), None, None),
        P("dp", ("inner", "outer")),
        P(),
        P(None, ("inner", "outer"), None),
    )
    return jax.shard_map(
        functools.partial(body, mesh.shape["outer"]),
        mesh=mesh,
        in_specs=placed,
        out_specs=(P("dp", ("inner", "outer")), P("dp", ("inner", "outer"), None)),
        check_vma=False,
    )
```

```python
import functools

import jax
import jax.numpy as jnp
from jax import lax
from jax.experimental import pallas as pl
from jax.experimental.pallas import tpu as pltpu
from jax.sharding import PartitionSpec as P

MESH = pl.DeviceIdType.MESH
F32 = jnp.float32
BF16 = jnp.bfloat16
PIECES = 16
AHEAD = 3
CYCLE = 3
EARLY = 2


def fused(n, pieces, partials, residual, gain, weight, stream_out, kv_out,
          mine, resid, gains, w, ybuf, rbuf, lbuf, g, tmp, acc, sq,
          loc, out_s, y_r, r_r, l_r, g_r):
    i = lax.axis_index("inner")
    o = lax.axis_index("outer")
    other = 1 - i
    rows, local = resid.shape
    width = gains.shape[1]
    half = n * local
    cols = local // pieces
    group = max(1, 256 // cols)
    early = sum(p % CYCLE < EARLY for p in range(pieces))
    to_y = {"inner": other}
    to_r = {"outer": jnp.minimum(o + 1, n - 1)}
    to_l = {"outer": jnp.maximum(o - 1, 0)}
    has_r = o < n - 1
    has_l = o > 0

    loads = [
        pltpu.make_async_copy(
            partials.at[0, :, pl.ds(pl.multiple_of(i * half, half), half)], mine, loc.at[0]
        ),
        pltpu.make_async_copy(residual, resid, loc.at[1]),
        pltpu.make_async_copy(gain, gains, loc.at[2]),
        pltpu.make_async_copy(weight, w, loc.at[3]),
    ]

    def remote(src, dst, ssem, rsem, to):
        return pltpu.make_async_remote_copy(
            src_ref=src, dst_ref=dst, send_sem=ssem, recv_sem=rsem,
            device_id=to, device_id_type=MESH,
        )

    def y_copy(d, p):
        at = pl.multiple_of(other * half + d * local + p * cols, cols)
        return remote(partials.at[0, :, pl.ds(at, cols)], ybuf.at[d, p],
                      out_s.at[0], y_r.at[d, p], to_y)

    def r_copy(d, p):
        return remote(rbuf.at[d, p], rbuf.at[d, p], out_s.at[1], r_r.at[d, p], to_r)

    def l_copy(d, p):
        return remote(lbuf.at[d, p], lbuf.at[d, p], out_s.at[1], l_r.at[d, p], to_l)

    def g_copy(t, p, kind, to):
        k = t * pieces + p
        return remote(g.at[k], g.at[k], out_s.at[kind], g_r.at[k], to)

    def inside(p):
        return (p >= 0) & (p < pieces)

    def is_early(p):
        return lax.rem(p, CYCLE) < EARLY

    def level_one(d, p):
        y_copy(d, p).wait_recv()
        at = pl.multiple_of(d * local + p * cols, cols)
        return mine[:, pl.ds(at, cols)].astype(F32) + ybuf[d, p].astype(F32)

    def skew(d):
        return jnp.where(d > o, o, jnp.where(d < o, n - 1 - o, n - 1))

    def send_y(s):
        for d in range(n):
            p = s - skew(d)

            @pl.when(inside(p))
            def _():
                y_copy(d, p).start()

    barrier = pltpu.get_barrier_semaphore()
    pl.semaphore_signal(barrier, inc=1, device_id=to_y, device_id_type=MESH)

    @pl.when(has_r)
    def _():
        pl.semaphore_signal(barrier, inc=1, device_id=to_r, device_id_type=MESH)

    @pl.when(has_l)
    def _():
        pl.semaphore_signal(barrier, inc=1, device_id=to_l, device_id_type=MESH)

    for load in loads[:3]:
        load.start()
    pl.semaphore_wait(barrier, 1 + has_r.astype(jnp.int32) + has_l.astype(jnp.int32))
    for s in range(AHEAD):
        send_y(jnp.int32(s))
    loads[3].start()
    acc[...] = jnp.zeros_like(acc)
    sq[...] = jnp.zeros_like(sq)
    for load in loads[:3]:
        load.wait()

    def passing(s):
        p = s - o

        @pl.when(inside(p) & has_r)
        def _():
            for d in reversed(range(n)):
                @pl.when(d > o)
                def _():
                    value = level_one(d, p)

                    @pl.when(has_l)
                    def _():
                        r_copy(d, p).wait_recv()
                        rbuf[d, p] = (value + rbuf[d, p].astype(F32)).astype(BF16)

                    @pl.when(jnp.logical_not(has_l))
                    def _():
                        rbuf[d, p] = value.astype(BF16)

                    r_copy(d, p).start()

        q = s - (n - 1 - o)

        @pl.when(inside(q) & has_l)
        def _():
            for d in range(n):
                @pl.when(d < o)
                def _():
                    value = level_one(d, q)

                    @pl.when(has_r)
                    def _():
                        l_copy(d, q).wait_recv()
                        lbuf[d, q] = (value + lbuf[d, q].astype(F32)).astype(BF16)

                    @pl.when(jnp.logical_not(has_r))
                    def _():
                        lbuf[d, q] = value.astype(BF16)

                    l_copy(d, q).start()

    def finish(s):
        p = s - (n - 1)

        @pl.when(inside(p))
        def _():
            at = pl.multiple_of(p * cols, cols)
            tmp[...] = level_one(o, p) + resid[:, pl.ds(at, cols)].astype(F32)

            @pl.when(has_l)
            def _():
                r_copy(o, p).wait_recv()
                tmp[...] += rbuf[o, p].astype(F32)

            @pl.when(has_r)
            def _():
                l_copy(o, p).wait_recv()
                tmp[...] += lbuf[o, p].astype(F32)

            value = tmp[...].astype(BF16)
            stream_out[:, pl.ds(at, cols)] = value
            me = i * n + o
            g[me * pieces + p] = value

            @pl.when(is_early(p))
            def _():
                g_copy(me, p, 2, to_y).start()

    def along(c, t, p, kind):
        @pl.when((c <= o) & has_r)
        def _():
            g_copy(t, p, kind, to_r).start()

        @pl.when((c >= o) & has_l)
        def _():
            g_copy(t, p, kind, to_l).start()

    def near(s):
        for c in range(n):
            p = s - (n - 1) - jnp.abs(o - c)
            t = i * n + c

            @pl.when(inside(p))
            def _():
                @pl.when(c != o)
                def _():
                    g_copy(t, p, 3, to_r).wait_recv()

                along(c, t, p, 3)

                @pl.when(jnp.logical_not(is_early(p)))
                def _():
                    g_copy(t, p, 2, to_y).start()

    def far(s):
        for c in range(n):
            p = s - n - jnp.abs(o - c)
            t = other * n + c

            @pl.when(inside(p))
            def _():
                g_copy(t, p, 2, to_y).wait_recv()

                @pl.when(is_early(p))
                def _():
                    along(c, t, p, 4)

    def multiply(s):
        @pl.loop(0, 2 * n)
        def _(k):
            away = (k >= n).astype(jnp.int32)
            c = k - away * n
            p = s - (n - 1) - jnp.abs(o - c) - away
            t = jnp.where(away > 0, other, i) * n + c

            @pl.when(inside(p) & (lax.rem(p, group) == group - 1))
            def _():
                first = p - (group - 1)
                at = pl.multiple_of(t * local + first * cols, group * cols)
                parts = [g[t * pieces + first + j] for j in range(group)]
                value = jnp.concatenate(parts, axis=1).astype(F32)
                square = value * value
                part = square[:, :128]
                for j in range(1, group * cols // 128):
                    part += square[:, j * 128:(j + 1) * 128]
                sq[...] += part
                scaled = (value * gains[:, pl.ds(at, group * cols)]).astype(BF16)
                acc[...] += jnp.dot(
                    scaled, w[pl.ds(at, group * cols), :], preferred_element_type=F32
                )

    @pl.loop(0, pieces + 2 * n - 1)
    def _(s):
        send_y(s + AHEAD)
        passing(s)
        finish(s)
        near(s)
        far(s)

        @pl.when(s == n - 1)
        def _():
            loads[3].wait()

        multiply(s)

    factor = lax.rsqrt(jnp.sum(sq[...], axis=1, keepdims=True) / width + 1e-05)
    kv_out[...] = (acc[...] * factor).astype(BF16)

    def sent(ref, kind):
        remote(ref, ref, out_s.at[kind], g_r.at[0], to_y).wait_send()

    sent(ybuf, 0)
    sent(rbuf.at[pl.ds(0, n - 1)], 1)
    sent(g.at[pl.ds(0, n * (pieces - early) + early)], 2)

    @pl.when(has_l & has_r)
    def _():
        sent(g.at[pl.ds(0, (n + 1) * pieces)], 3)
        sent(g.at[pl.ds(0, (n + 1) * early)], 4)

    @pl.when(jnp.logical_not(has_l & has_r))
    def _():
        sent(g.at[pl.ds(0, pieces)], 3)
        sent(g.at[pl.ds(0, early)], 4)


def body(n, partials, residual, norm_gain, kv_weight):
    rows, local = residual.shape
    width = norm_gain.shape[0]
    heads_local, pair = kv_weight.shape[1:]
    pieces = PIECES
    cols = local // pieces
    wide = heads_local * pair
    dma = pltpu.SemaphoreType.DMA
    vmem = pltpu.VMEM
    stream, kv = pl.pallas_call(
        functools.partial(fused, n, pieces),
        out_shape=(
            jax.ShapeDtypeStruct((rows, local), BF16),
            jax.ShapeDtypeStruct((rows, wide), BF16),
        ),
        in_specs=[pl.BlockSpec(memory_space=pl.ANY)] * 4,
        out_specs=(pl.BlockSpec(memory_space=pltpu.VMEM),) * 2,
        scratch_shapes=[
            vmem((rows, n * local), BF16),
            vmem((rows, local), BF16),
            vmem((1, width), F32),
            vmem((width, wide), BF16),
            vmem((n, pieces, rows, cols), BF16),
            vmem((n, pieces, rows, cols), BF16),
            vmem((n, pieces, rows, cols), BF16),
            vmem((2 * n * pieces, rows, cols), BF16),
            vmem((rows, cols), F32),
            vmem((rows, wide), F32),
            vmem((rows, 128), F32),
            dma((4,)),
            dma((5,)),
            dma((n, pieces)),
            dma((n, pieces)),
            dma((n, pieces)),
            dma((2 * n * pieces,)),
        ],
        compiler_params=pltpu.CompilerParams(
            collective_id=0, has_side_effects=True, vmem_limit_bytes=60 * 1024 * 1024
        ),
        cost_estimate=pl.CostEstimate(
            flops=2 * rows * width * wide,
            bytes_accessed=2 * (rows * width + width * wide),
            transcendentals=rows,
        ),
    )(partials, residual, norm_gain.reshape(1, width), kv_weight.reshape(width, wide))
    return stream, kv.reshape(rows, heads_local, pair)


def solution(mesh):
    placed = (
        P(("dp", "inner", "outer"), None, None),
        P("dp", ("inner", "outer")),
        P(),
        P(None, ("inner", "outer"), None),
    )
    return jax.shard_map(
        functools.partial(body, mesh.shape["outer"]),
        mesh=mesh,
        in_specs=placed,
        out_specs=(P("dp", ("inner", "outer")), P("dp", ("inner", "outer"), None)),
        check_vma=False,
    )
```

```python
import functools

import jax
import jax.numpy as jnp
from jax import lax
from jax.experimental import pallas as pl
from jax.experimental.pallas import tpu as pltpu
from jax.sharding import PartitionSpec as P

MESH = pl.DeviceIdType.MESH
F32 = jnp.float32
BF16 = jnp.bfloat16
PIECES = 16
AHEAD = 3
CYCLE = 3
EARLY = 1


def fused(n, pieces, partials, residual, gain, weight, stream_out, kv_out,
          mine, resid, gains, w, ybuf, z1_out, z1_in, z2_out, z2_in, g, acc, sq,
          loc, out_s, y_r, hop_r):
    i = lax.axis_index("inner")
    o = lax.axis_index("outer")
    other = 1 - i
    par = lax.rem(o, 2)
    high = o // 2
    rows, local = resid.shape
    width = gains.shape[1]
    half = n * local
    cols = local // pieces
    group = max(1, 256 // cols)
    early = sum(p % CYCLE < EARLY for p in range(pieces))
    to_y = {"inner": other}
    to_1 = {"outer": o + 1 - 2 * par}
    to_2 = {"outer": o + 2 - 4 * high}

    loads = [
        pltpu.make_async_copy(
            partials.at[0, :, pl.ds(pl.multiple_of(i * half, half), half)], mine, loc.at[0]
        ),
        pltpu.make_async_copy(residual, resid, loc.at[1]),
        pltpu.make_async_copy(gain, gains, loc.at[2]),
        pltpu.make_async_copy(weight, w, loc.at[3]),
    ]

    def remote(src, dst, ssem, rsem, to):
        return pltpu.make_async_remote_copy(
            src_ref=src, dst_ref=dst, send_sem=ssem, recv_sem=rsem,
            device_id=to, device_id_type=MESH,
        )

    def y_copy(d, p):
        at = pl.multiple_of(other * half + d * local + p * cols, cols)
        return remote(partials.at[0, :, pl.ds(at, cols)], ybuf.at[d, p],
                      out_s.at[0], y_r.at[d, p], to_y)

    def z1_copy(p):
        return remote(z1_out.at[p], z1_in.at[p], out_s.at[1], hop_r.at[0, p], to_1)

    def z2_copy(p):
        return remote(z2_out.at[p], z2_in.at[p], out_s.at[2], hop_r.at[1, p], to_2)

    def place(side, odd, p):
        return ((side * 2 + odd) * pieces + p) * 2

    def one(side, odd, up, p, kind, hop, to):
        ref = g.at[pl.ds(place(side, odd, p) + up, 1)]
        return remote(ref, ref, out_s.at[kind], hop_r.at[hop, p], to)

    def two(side, odd, p, kind, hop, to):
        ref = g.at[pl.ds(place(side, odd, p), 2)]
        return remote(ref, ref, out_s.at[kind], hop_r.at[hop, p], to)

    def inside(p):
        return (p >= 0) & (p < pieces)

    def is_early(p):
        return lax.rem(p, CYCLE) < EARLY

    def level_one(d, p):
        at = pl.multiple_of(d * local + p * cols, cols)
        return mine[:, pl.ds(at, cols)].astype(F32) + ybuf[d, p].astype(F32)

    def send_y(s):
        @pl.when(inside(s))
        def _():
            for k in range(2):
                y_copy(2 * k + 1 - par, s).start()

        @pl.when(inside(s - 1))
        def _():
            for k in range(2):
                y_copy(2 * k + par, s - 1).start()

    barrier = pltpu.get_barrier_semaphore()
    for to in (to_y, to_1, to_2):
        pl.semaphore_signal(barrier, inc=1, device_id=to, device_id_type=MESH)
    for load in loads[:3]:
        load.start()
    pl.semaphore_wait(barrier, 3)
    for s in range(AHEAD):
        send_y(jnp.int32(s))
    loads[3].start()
    acc[...] = jnp.zeros_like(acc)
    sq[...] = jnp.zeros_like(sq)
    for load in loads[:3]:
        load.wait()

    def stage_0(p):
        for k in range(2):
            d = 2 * k + 1 - par
            y_copy(d, p).wait_recv()
            z1_out[p, k] = level_one(d, p).astype(BF16)
        z1_copy(p).start()

    def stage_1(p):
        for k in range(2):
            y_copy(2 * k + par, p).wait_recv()
        z1_copy(p).wait_recv()
        up = 1 - high
        value = level_one(2 * up + par, p) + z1_in[p, up].astype(F32)
        z2_out[p] = value.astype(BF16)
        z2_copy(p).start()

    def stage_2(p):
        z2_copy(p).wait_recv()
        at = pl.multiple_of(p * cols, cols)
        value = level_one(o, p) + z1_in[p, high].astype(F32) + z2_in[p].astype(F32)
        value = (value + resid[:, pl.ds(at, cols)].astype(F32)).astype(BF16)
        stream_out[:, pl.ds(at, cols)] = value
        g[place(i, par, p) + high] = value
        one(i, par, high, p, 3, 2, to_2).start()

        @pl.when(is_early(p))
        def _():
            one(i, par, high, p, 5, 4, to_y).start()

    def stage_3(p):
        one(i, par, 1 - high, p, 3, 2, to_2).wait_recv()
        two(i, par, p, 4, 3, to_1).start()

        @pl.when(is_early(p))
        def _():
            one(other, par, high, p, 5, 4, to_y).wait_recv()
            one(other, par, high, p, 6, 6, to_2).start()

        @pl.when(jnp.logical_not(is_early(p)))
        def _():
            two(i, par, p, 5, 4, to_y).start()

    def stage_4(p):
        two(i, 1 - par, p, 4, 3, to_1).wait_recv()

        @pl.when(is_early(p))
        def _():
            one(other, par, 1 - high, p, 6, 6, to_2).wait_recv()
            two(other, par, p, 7, 7, to_1).start()

        @pl.when(jnp.logical_not(is_early(p)))
        def _():
            two(i, 1 - par, p, 5, 5, to_y).start()
            two(other, par, p, 5, 4, to_y).wait_recv()

    def stage_5(p):
        @pl.when(is_early(p))
        def _():
            two(other, 1 - par, p, 7, 7, to_1).wait_recv()

        @pl.when(jnp.logical_not(is_early(p)))
        def _():
            two(other, 1 - par, p, 5, 5, to_y).wait_recv()

    def multiply(s):
        @pl.loop(0, 4)
        def _(k):
            away = k // 2
            flip = lax.rem(k, 2)
            side = i + away * (1 - 2 * i)
            odd = par + flip * (1 - 2 * par)
            p = s - 3 - away - flip

            @pl.when(inside(p) & (lax.rem(p, group) == group - 1))
            def _():
                first = p - (group - 1)
                total = acc[...]
                squares = sq[...]
                for up in range(2):
                    t = side * n + 2 * up + odd
                    at = pl.multiple_of(t * local + first * cols, group * cols)
                    parts = [g[place(side, odd, first + j) + up] for j in range(group)]
                    value = jnp.concatenate(parts, axis=1).astype(F32)
                    square = value * value
                    for j in range(group * cols // 128):
                        squares += square[:, j * 128:(j + 1) * 128]
                    scaled = (value * gains[:, pl.ds(at, group * cols)]).astype(BF16)
                    total += jnp.dot(
                        scaled, w[pl.ds(at, group * cols), :], preferred_element_type=F32
                    )
                sq[...] = squares
                acc[...] = total

    @pl.loop(0, pieces + 5)
    def _(s):
        send_y(s + AHEAD)
        for k, stage in enumerate((stage_0, stage_1, stage_2, stage_3, stage_4, stage_5)):
            @pl.when(inside(s - k))
            def _():
                stage(s - k)

        @pl.when(s == 3)
        def _():
            loads[3].wait()

        multiply(s)

    factor = lax.rsqrt(jnp.sum(sq[...], axis=1, keepdims=True) / width + 1e-05)
    kv_out[...] = (acc[...] * factor).astype(BF16)

    def sent(ref, kind):
        remote(ref, ref, out_s.at[kind], hop_r.at[0, 0], to_y).wait_send()

    sent(ybuf, 0)
    sent(z1_out, 1)
    sent(z2_out, 2)
    sent(g.at[pl.ds(0, pieces)], 3)
    sent(g.at[pl.ds(0, 2 * pieces)], 4)
    sent(g.at[pl.ds(0, 4 * (pieces - early) + early)], 5)
    sent(g.at[pl.ds(0, early)], 6)
    sent(g.at[pl.ds(0, 2 * early)], 7)


def body(n, partials, residual, norm_gain, kv_weight):
    rows, local = residual.shape
    width = norm_gain.shape[0]
    heads_local, pair = kv_weight.shape[1:]
    pieces = PIECES
    cols = local // pieces
    wide = heads_local * pair
    dma = pltpu.SemaphoreType.DMA
    vmem = pltpu.VMEM
    stream, kv = pl.pallas_call(
        functools.partial(fused, n, pieces),
        out_shape=(
            jax.ShapeDtypeStruct((rows, local), BF16),
            jax.ShapeDtypeStruct((rows, wide), BF16),
        ),
        in_specs=[pl.BlockSpec(memory_space=pl.ANY)] * 4,
        out_specs=(pl.BlockSpec(memory_space=pltpu.VMEM),) * 2,
        scratch_shapes=[
            vmem((rows, n * local), BF16),
            vmem((rows, local), BF16),
            vmem((1, width), F32),
            vmem((width, wide), BF16),
            vmem((n, pieces, rows, cols), BF16),
            vmem((pieces, 2, rows, cols), BF16),
            vmem((pieces, 2, rows, cols), BF16),
            vmem((pieces, rows, cols), BF16),
            vmem((pieces, rows, cols), BF16),
            vmem((2 * n * pieces, rows, cols), BF16),
            vmem((rows, wide), F32),
            vmem((rows, 128), F32),
            dma((4,)),
            dma((8,)),
            dma((n, pieces)),
            dma((8, pieces)),
        ],
        compiler_params=pltpu.CompilerParams(
            collective_id=0, has_side_effects=True, vmem_limit_bytes=60 * 1024 * 1024
        ),
        cost_estimate=pl.CostEstimate(
            flops=2 * rows * width * wide,
            bytes_accessed=2 * (rows * width + width * wide),
            transcendentals=rows,
        ),
    )(partials, residual, norm_gain.reshape(1, width), kv_weight.reshape(width, wide))
    return stream, kv.reshape(rows, heads_local, pair)


def solution(mesh):
    placed = (
        P(("dp", "inner", "outer"), None, None),
        P("dp", ("inner", "outer")),
        P(),
        P(None, ("inner", "outer"), None),
    )
    return jax.shard_map(
        functools.partial(body, mesh.shape["outer"]),
        mesh=mesh,
        in_specs=placed,
        out_specs=(P("dp", ("inner", "outer")), P("dp", ("inner", "outer"), None)),
        check_vma=False,
    )
```

```python
import functools

import jax
import jax.numpy as jnp
from jax import lax
from jax.experimental import pallas as pl
from jax.experimental.pallas import tpu as pltpu
from jax.sharding import PartitionSpec as P

MESH = pl.DeviceIdType.MESH
F32 = jnp.float32
BF16 = jnp.bfloat16
PIECES = 16
AHEAD = 4
SLACK = 2
CYCLE = 3
EARLY = 1


def fused(n, pieces, partials, residual, gain, weight, stream_out, kv_out,
          mine, resid, gains, w, ybuf, z1_out, z1_in, z2_out, z2_in, g, acc, sq,
          loc, out_s, y_r, hop_r):
    i = lax.axis_index("inner")
    o = lax.axis_index("outer")
    other = 1 - i
    par = lax.rem(o, 2)
    high = o // 2
    rows, local = resid.shape
    width = gains.shape[1]
    half = n * local
    cols = local // pieces
    group = max(1, 256 // cols)
    early = sum(p % CYCLE < EARLY for p in range(pieces))
    to_y = {"inner": other}
    to_1 = {"outer": o + 1 - 2 * par}
    to_2 = {"outer": o + 2 - 4 * high}

    loads = [
        pltpu.make_async_copy(
            partials.at[0, :, pl.ds(pl.multiple_of(i * half, half), half)], mine, loc.at[0]
        ),
        pltpu.make_async_copy(residual, resid, loc.at[1]),
        pltpu.make_async_copy(gain, gains, loc.at[2]),
        pltpu.make_async_copy(weight, w, loc.at[3]),
    ]

    def remote(src, dst, ssem, rsem, to):
        return pltpu.make_async_remote_copy(
            src_ref=src, dst_ref=dst, send_sem=ssem, recv_sem=rsem,
            device_id=to, device_id_type=MESH,
        )

    def y_copy(d, p):
        at = pl.multiple_of(other * half + d * local + p * cols, cols)
        return remote(partials.at[0, :, pl.ds(at, cols)], ybuf.at[d, p],
                      out_s.at[0], y_r.at[d, p], to_y)

    def z1_copy(p):
        return remote(z1_out.at[p], z1_in.at[p], out_s.at[1], hop_r.at[0, p], to_1)

    def z2_copy(p):
        return remote(z2_out.at[p], z2_in.at[p], out_s.at[2], hop_r.at[1, p], to_2)

    def place(side, odd, p):
        return ((side * 2 + odd) * pieces + p) * 2

    def one(side, odd, up, p, kind, hop, to):
        ref = g.at[pl.ds(place(side, odd, p) + up, 1)]
        return remote(ref, ref, out_s.at[kind], hop_r.at[hop, p], to)

    def two(side, odd, p, kind, hop, to):
        ref = g.at[pl.ds(place(side, odd, p), 2)]
        return remote(ref, ref, out_s.at[kind], hop_r.at[hop, p], to)

    def inside(p):
        return (p >= 0) & (p < pieces)

    def is_early(p):
        return lax.rem(p, CYCLE) < EARLY

    def level_one(d, p):
        at = pl.multiple_of(d * local + p * cols, cols)
        return mine[:, pl.ds(at, cols)].astype(F32) + ybuf[d, p].astype(F32)

    def send_y(s):
        @pl.when(inside(s))
        def _():
            for k in range(2):
                y_copy(2 * k + 1 - par, s).start()

        @pl.when(inside(s - SLACK))
        def _():
            for k in range(2):
                y_copy(2 * k + par, s - SLACK).start()

    barrier = pltpu.get_barrier_semaphore()
    for to in (to_y, to_1, to_2):
        pl.semaphore_signal(barrier, inc=1, device_id=to, device_id_type=MESH)
    for load in loads[:3]:
        load.start()
    pl.semaphore_wait(barrier, 3)
    for s in range(AHEAD):
        send_y(jnp.int32(s))
    loads[3].start()
    acc[...] = jnp.zeros_like(acc)
    sq[...] = jnp.zeros_like(sq)
    for load in loads[:3]:
        load.wait()

    def stage_0(p):
        for k in range(2):
            d = 2 * k + 1 - par
            y_copy(d, p).wait_recv()
            z1_out[p, k] = level_one(d, p).astype(BF16)
        z1_copy(p).start()

    def stage_1(p):
        for k in range(2):
            y_copy(2 * k + par, p).wait_recv()
        z1_copy(p).wait_recv()
        up = 1 - high
        value = level_one(2 * up + par, p) + z1_in[p, up].astype(F32)
        z2_out[p] = value.astype(BF16)
        z2_copy(p).start()

    def stage_2(p):
        z2_copy(p).wait_recv()
        at = pl.multiple_of(p * cols, cols)
        value = level_one(o, p) + z1_in[p, high].astype(F32) + z2_in[p].astype(F32)
        value = (value + resid[:, pl.ds(at, cols)].astype(F32)).astype(BF16)
        stream_out[:, pl.ds(at, cols)] = value
        g[place(i, par, p) + high] = value
        one(i, par, high, p, 3, 2, to_2).start()

        @pl.when(is_early(p))
        def _():
            one(i, par, high, p, 5, 4, to_y).start()

    def stage_3(p):
        one(i, par, 1 - high, p, 3, 2, to_2).wait_recv()
        two(i, par, p, 4, 3, to_1).start()

        @pl.when(is_early(p))
        def _():
            one(other, par, high, p, 5, 4, to_y).wait_recv()
            one(other, par, high, p, 6, 6, to_2).start()

        @pl.when(jnp.logical_not(is_early(p)))
        def _():
            two(i, par, p, 5, 4, to_y).start()

    def stage_4(p):
        two(i, 1 - par, p, 4, 3, to_1).wait_recv()

        @pl.when(is_early(p))
        def _():
            one(other, par, 1 - high, p, 6, 6, to_2).wait_recv()
            two(other, par, p, 7, 7, to_1).start()

        @pl.when(jnp.logical_not(is_early(p)))
        def _():
            two(i, 1 - par, p, 5, 5, to_y).start()
            two(other, par, p, 5, 4, to_y).wait_recv()

    def stage_5(p):
        @pl.when(is_early(p))
        def _():
            two(other, 1 - par, p, 7, 7, to_1).wait_recv()

        @pl.when(jnp.logical_not(is_early(p)))
        def _():
            two(other, 1 - par, p, 5, 5, to_y).wait_recv()

    def multiply(s):
        @pl.loop(0, 4)
        def _(k):
            away = k // 2
            flip = lax.rem(k, 2)
            side = i + away * (1 - 2 * i)
            odd = par + flip * (1 - 2 * par)
            p = s - SLACK * (3 + away + flip)

            @pl.when(inside(p) & (lax.rem(p, group) == group - 1))
            def _():
                first = p - (group - 1)
                total = acc[...]
                squares = sq[...]
                for up in range(2):
                    t = side * n + 2 * up + odd
                    at = pl.multiple_of(t * local + first * cols, group * cols)
                    parts = [g[place(side, odd, first + j) + up] for j in range(group)]
                    value = jnp.concatenate(parts, axis=1).astype(F32)
                    square = value * value
                    for j in range(group * cols // 128):
                        squares += square[:, j * 128:(j + 1) * 128]
                    scaled = (value * gains[:, pl.ds(at, group * cols)]).astype(BF16)
                    total += jnp.dot(
                        scaled, w[pl.ds(at, group * cols), :], preferred_element_type=F32
                    )
                sq[...] = squares
                acc[...] = total

    @pl.loop(0, pieces + 5 * SLACK)
    def _(s):
        send_y(s + AHEAD)
        for k, stage in enumerate((stage_0, stage_1, stage_2, stage_3, stage_4, stage_5)):
            @pl.when(inside(s - SLACK * k))
            def _():
                stage(s - SLACK * k)

        @pl.when(s == 3 * SLACK)
        def _():
            loads[3].wait()

        multiply(s)

    factor = lax.rsqrt(jnp.sum(sq[...], axis=1, keepdims=True) / width + 1e-05)
    kv_out[...] = (acc[...] * factor).astype(BF16)

    def sent(ref, kind):
        remote(ref, ref, out_s.at[kind], hop_r.at[0, 0], to_y).wait_send()

    sent(ybuf, 0)
    sent(z1_out, 1)
    sent(z2_out, 2)
    sent(g.at[pl.ds(0, pieces)], 3)
    sent(g.at[pl.ds(0, 2 * pieces)], 4)
    sent(g.at[pl.ds(0, 4 * (pieces - early) + early)], 5)
    sent(g.at[pl.ds(0, early)], 6)
    sent(g.at[pl.ds(0, 2 * early)], 7)


def body(n, partials, residual, norm_gain, kv_weight):
    rows, local = residual.shape
    width = norm_gain.shape[0]
    heads_local, pair = kv_weight.shape[1:]
    pieces = PIECES
    cols = local // pieces
    wide = heads_local * pair
    dma = pltpu.SemaphoreType.DMA
    vmem = pltpu.VMEM
    stream, kv = pl.pallas_call(
        functools.partial(fused, n, pieces),
        out_shape=(
            jax.ShapeDtypeStruct((rows, local), BF16),
            jax.ShapeDtypeStruct((rows, wide), BF16),
        ),
        in_specs=[pl.BlockSpec(memory_space=pl.ANY)] * 4,
        out_specs=(pl.BlockSpec(memory_space=pltpu.VMEM),) * 2,
        scratch_shapes=[
            vmem((rows, n * local), BF16),
            vmem((rows, local), BF16),
            vmem((1, width), F32),
            vmem((width, wide), BF16),
            vmem((n, pieces, rows, cols), BF16),
            vmem((pieces, 2, rows, cols), BF16),
            vmem((pieces, 2, rows, cols), BF16),
            vmem((pieces, rows, cols), BF16),
            vmem((pieces, rows, cols), BF16),
            vmem((2 * n * pieces, rows, cols), BF16),
            vmem((rows, wide), F32),
            vmem((rows, 128), F32),
            dma((4,)),
            dma((8,)),
            dma((n, pieces)),
            dma((8, pieces)),
        ],
        compiler_params=pltpu.CompilerParams(
            collective_id=0, has_side_effects=True, vmem_limit_bytes=60 * 1024 * 1024
        ),
        cost_estimate=pl.CostEstimate(
            flops=2 * rows * width * wide,
            bytes_accessed=2 * (rows * width + width * wide),
            transcendentals=rows,
        ),
    )(partials, residual, norm_gain.reshape(1, width), kv_weight.reshape(width, wide))
    return stream, kv.reshape(rows, heads_local, pair)


def solution(mesh):
    placed = (
        P(("dp", "inner", "outer"), None, None),
        P("dp", ("inner", "outer")),
        P(),
        P(None, ("inner", "outer"), None),
    )
    return jax.shard_map(
        functools.partial(body, mesh.shape["outer"]),
        mesh=mesh,
        in_specs=placed,
        out_specs=(P("dp", ("inner", "outer")), P("dp", ("inner", "outer"), None)),
        check_vma=False,
    )
```

```python
import functools

import jax
import jax.numpy as jnp
from jax import lax
from jax.experimental import pallas as pl
from jax.experimental.pallas import tpu as pltpu
from jax.sharding import PartitionSpec as P

MESH = pl.DeviceIdType.MESH
F32 = jnp.float32
BF16 = jnp.bfloat16
PIECES = 16
AHEAD = 3
CYCLE = 5
EARLY = 2


def fused(n, pieces, partials, residual, gain, weight, stream_out, kv_out,
          mine, resid, gains, w, ybuf, zbuf, rbuf, lbuf, g, tmp, acc, sq,
          loc, out_s, y_r, r_r, l_r, g_r):
    i = lax.axis_index("inner")
    o = lax.axis_index("outer")
    other = 1 - i
    rows, local = resid.shape
    width = gains.shape[1]
    half = n * local
    cols = local // pieces
    group = max(1, 256 // cols)
    early = sum((2 * p + 2) % CYCLE < EARLY for p in range(pieces))
    to_y = {"inner": other}
    to_r = {"outer": jnp.minimum(o + 1, n - 1)}
    to_l = {"outer": jnp.maximum(o - 1, 0)}
    has_r = o < n - 1
    has_l = o > 0

    loads = [
        pltpu.make_async_copy(partials.at[0], mine, loc.at[0]),
        pltpu.make_async_copy(residual, resid, loc.at[1]),
        pltpu.make_async_copy(gain, gains, loc.at[2]),
        pltpu.make_async_copy(weight, w, loc.at[3]),
    ]

    def remote(src, dst, ssem, rsem, to):
        return pltpu.make_async_remote_copy(
            src_ref=src, dst_ref=dst, send_sem=ssem, recv_sem=rsem,
            device_id=to, device_id_type=MESH,
        )

    def y_copy(d, p):
        at = pl.multiple_of(other * half + d * local + p * cols, cols)
        return remote(partials.at[0, :, pl.ds(at, cols)], ybuf.at[d, p],
                      out_s.at[0], y_r.at[d, p], to_y)

    def sum_copy(p):
        return remote(zbuf.at[p], ybuf.at[o, p], out_s.at[0], y_r.at[o, p], to_y)

    def r_copy(side, d, p):
        ref = rbuf.at[side, d, p]
        return remote(ref, ref, out_s.at[1], r_r.at[side, d, p], to_r)

    def l_copy(side, d, p):
        ref = lbuf.at[side, d, p]
        return remote(ref, ref, out_s.at[1], l_r.at[side, d, p], to_l)

    def g_copy(t, p, kind, to):
        k = t * pieces + p
        return remote(g.at[k], g.at[k], out_s.at[kind], g_r.at[k], to)

    def inside(p):
        return (p >= 0) & (p < pieces)

    def is_early(p):
        return lax.rem(2 * p + 2, CYCLE) < EARLY

    def part(side, d, p):
        at = pl.multiple_of(side * half + d * local + p * cols, cols)
        return mine[:, pl.ds(at, cols)].astype(F32)

    def level_one(d, p):
        y_copy(d, p).wait_recv()
        return part(i, d, p) + ybuf[d, p].astype(F32)

    def skew(d):
        return jnp.where(d > o, o, jnp.where(d < o, n - 1 - o, n - 1))

    def send_y(s):
        for d in range(n):
            p = s - skew(d)

            @pl.when(inside(p) & jnp.logical_not(is_early(p)))
            def _():
                y_copy(d, p).start()

    barrier = pltpu.get_barrier_semaphore()
    pl.semaphore_signal(barrier, inc=1, device_id=to_y, device_id_type=MESH)

    @pl.when(has_r)
    def _():
        pl.semaphore_signal(barrier, inc=1, device_id=to_r, device_id_type=MESH)

    @pl.when(has_l)
    def _():
        pl.semaphore_signal(barrier, inc=1, device_id=to_l, device_id_type=MESH)

    for load in loads[:3]:
        load.start()
    pl.semaphore_wait(barrier, 1 + has_r.astype(jnp.int32) + has_l.astype(jnp.int32))
    for s in range(AHEAD - 1):
        send_y(jnp.int32(s))
    loads[3].start()
    acc[...] = jnp.zeros_like(acc)
    sq[...] = jnp.zeros_like(sq)
    for load in loads[:3]:
        load.wait()

    def hand_on(value, buf, copy, has_before, side, d, p):
        @pl.when(has_before)
        def _():
            copy(side, d, p).wait_recv()
            buf[side, d, p] = (value + buf[side, d, p].astype(F32)).astype(BF16)

        @pl.when(jnp.logical_not(has_before))
        def _():
            buf[side, d, p] = value.astype(BF16)

        copy(side, d, p).start()

    def passing(s):
        for lead in range(2):
            p = s - o + lead
            mode = is_early(p) if lead else jnp.logical_not(is_early(p))

            @pl.when(inside(p) & has_r & mode)
            def _():
                for d in reversed(range(n)):
                    @pl.when(d > o)
                    def _():
                        if lead:
                            for side in range(2):
                                hand_on(part(side, d, p), rbuf, r_copy, has_l, side, d, p)
                        else:
                            hand_on(level_one(d, p), rbuf, r_copy, has_l, i, d, p)

        for lead in range(2):
            q = s - (n - 1 - o) + lead
            mode = is_early(q) if lead else jnp.logical_not(is_early(q))

            @pl.when(inside(q) & has_l & mode)
            def _():
                for d in range(n):
                    @pl.when(d < o)
                    def _():
                        if lead:
                            for side in range(2):
                                hand_on(part(side, d, q), lbuf, l_copy, has_r, side, d, q)
                        else:
                            hand_on(level_one(d, q), lbuf, l_copy, has_r, i, d, q)

    def add_passed(side, p):
        @pl.when(has_l)
        def _():
            r_copy(side, o, p).wait_recv()
            tmp[...] += rbuf[side, o, p].astype(F32)

        @pl.when(has_r)
        def _():
            l_copy(side, o, p).wait_recv()
            tmp[...] += lbuf[side, o, p].astype(F32)

    def finish(s):
        early_p = s - (n - 1) + 1

        @pl.when(inside(early_p) & is_early(early_p))
        def _():
            tmp[...] = part(other, o, early_p)
            add_passed(other, early_p)
            zbuf[early_p] = tmp[...].astype(BF16)
            sum_copy(early_p).start()

        p = s - (n - 1)

        @pl.when(inside(p))
        def _():
            at = pl.multiple_of(p * cols, cols)
            tmp[...] = level_one(o, p) + resid[:, pl.ds(at, cols)].astype(F32)
            add_passed(i, p)
            value = tmp[...].astype(BF16)
            stream_out[:, pl.ds(at, cols)] = value
            me = i * n + o
            g[me * pieces + p] = value

            @pl.when(is_early(p))
            def _():
                g_copy(me, p, 2, to_y).start()

    def along(c, t, p, kind):
        @pl.when((c <= o) & has_r)
        def _():
            g_copy(t, p, kind, to_r).start()

        @pl.when((c >= o) & has_l)
        def _():
            g_copy(t, p, kind, to_l).start()

    def near(s):
        for c in range(n):
            p = s - (n - 1) - jnp.abs(o - c)
            t = i * n + c

            @pl.when(inside(p))
            def _():
                @pl.when(c != o)
                def _():
                    g_copy(t, p, 3, to_r).wait_recv()

                along(c, t, p, 3)

                @pl.when(jnp.logical_not(is_early(p)))
                def _():
                    g_copy(t, p, 2, to_y).start()

    def far(s):
        for c in range(n):
            p = s - n - jnp.abs(o - c)
            t = other * n + c

            @pl.when(inside(p))
            def _():
                g_copy(t, p, 2, to_y).wait_recv()

                @pl.when(is_early(p))
                def _():
                    along(c, t, p, 4)

    def multiply(s):
        @pl.loop(0, 2 * n)
        def _(k):
            away = (k >= n).astype(jnp.int32)
            c = k - away * n
            p = s - (n - 1) - jnp.abs(o - c) - away
            t = jnp.where(away > 0, other, i) * n + c

            @pl.when(inside(p) & (lax.rem(p, group) == group - 1))
            def _():
                first = p - (group - 1)
                at = pl.multiple_of(t * local + first * cols, group * cols)
                parts = [g[t * pieces + first + j] for j in range(group)]
                value = jnp.concatenate(parts, axis=1).astype(F32)
                square = value * value
                part = square[:, :128]
                for j in range(1, group * cols // 128):
                    part += square[:, j * 128:(j + 1) * 128]
                sq[...] += part
                scaled = (value * gains[:, pl.ds(at, group * cols)]).astype(BF16)
                acc[...] += jnp.dot(
                    scaled, w[pl.ds(at, group * cols), :], preferred_element_type=F32
                )

    @pl.loop(0, pieces + 2 * n)
    def _(step):
        s = step - 1
        send_y(s + AHEAD)
        passing(s)
        finish(s)
        near(s)
        far(s)

        @pl.when(s == n - 1)
        def _():
            loads[3].wait()

        multiply(s)

    factor = lax.rsqrt(jnp.sum(sq[...], axis=1, keepdims=True) / width + 1e-05)
    kv_out[...] = (acc[...] * factor).astype(BF16)

    def sent(ref, kind):
        remote(ref, ref, out_s.at[kind], g_r.at[0], to_y).wait_send()

    sent(g.at[pl.ds(0, n * (pieces - early) + early)], 0)
    sent(g.at[pl.ds(0, (n - 1) * (pieces + early))], 1)
    sent(g.at[pl.ds(0, n * (pieces - early) + early)], 2)

    @pl.when(has_l & has_r)
    def _():
        sent(g.at[pl.ds(0, (n + 1) * pieces)], 3)
        sent(g.at[pl.ds(0, (n + 1) * early)], 4)

    @pl.when(jnp.logical_not(has_l & has_r))
    def _():
        sent(g.at[pl.ds(0, pieces)], 3)
        sent(g.at[pl.ds(0, early)], 4)


def body(n, partials, residual, norm_gain, kv_weight):
    rows, local = residual.shape
    width = norm_gain.shape[0]
    heads_local, pair = kv_weight.shape[1:]
    pieces = PIECES
    cols = local // pieces
    wide = heads_local * pair
    dma = pltpu.SemaphoreType.DMA
    vmem = pltpu.VMEM
    stream, kv = pl.pallas_call(
        functools.partial(fused, n, pieces),
        out_shape=(
            jax.ShapeDtypeStruct((rows, local), BF16),
            jax.ShapeDtypeStruct((rows, wide), BF16),
        ),
        in_specs=[pl.BlockSpec(memory_space=pl.ANY)] * 4,
        out_specs=(pl.BlockSpec(memory_space=pltpu.VMEM),) * 2,
        scratch_shapes=[
            vmem((rows, width), BF16),
            vmem((rows, local), BF16),
            vmem((1, width), F32),
            vmem((width, wide), BF16),
            vmem((n, pieces, rows, cols), BF16),
            vmem((pieces, rows, cols), BF16),
            vmem((2, n, pieces, rows, cols), BF16),
            vmem((2, n, pieces, rows, cols), BF16),
            vmem((2 * n * pieces, rows, cols), BF16),
            vmem((rows, cols), F32),
            vmem((rows, wide), F32),
            vmem((rows, 128), F32),
            dma((4,)),
            dma((5,)),
            dma((n, pieces)),
            dma((2, n, pieces)),
            dma((2, n, pieces)),
            dma((2 * n * pieces,)),
        ],
        compiler_params=pltpu.CompilerParams(
            collective_id=0, has_side_effects=True, vmem_limit_bytes=60 * 1024 * 1024
        ),
        cost_estimate=pl.CostEstimate(
            flops=2 * rows * width * wide,
            bytes_accessed=2 * (rows * width + width * wide),
            transcendentals=rows,
        ),
    )(partials, residual, norm_gain.reshape(1, width), kv_weight.reshape(width, wide))
    return stream, kv.reshape(rows, heads_local, pair)


def solution(mesh):
    placed = (
        P(("dp", "inner", "outer"), None, None),
        P("dp", ("inner", "outer")),
        P(),
        P(None, ("inner", "outer"), None),
    )
    return jax.shard_map(
        functools.partial(body, mesh.shape["outer"]),
        mesh=mesh,
        in_specs=placed,
        out_specs=(P("dp", ("inner", "outer")), P("dp", ("inner", "outer"), None)),
        check_vma=False,
    )
```

```python
import functools

import jax
import jax.numpy as jnp
from jax import lax
from jax.experimental import pallas as pl
from jax.experimental.pallas import tpu as pltpu
from jax.sharding import PartitionSpec as P

MESH = pl.DeviceIdType.MESH
F32 = jnp.float32
BF16 = jnp.bfloat16
PIECES = 8
AHEAD = 2
CYCLE = 2
EARLY = 1


def fused(n, pieces, partials, residual, gain, weight, stream_out, kv_out,
          mine, resid, gains, w, ybuf, rbuf, lbuf, g, tmp, acc, sq,
          loc, out_s, y_r, r_r, l_r, g_r):
    i = lax.axis_index("inner")
    o = lax.axis_index("outer")
    other = 1 - i
    rows, local = resid.shape
    width = gains.shape[1]
    half = n * local
    cols = local // pieces
    group = max(1, 256 // cols)
    early = sum(p % CYCLE < EARLY for p in range(pieces))
    to_y = {"inner": other}
    to_r = {"outer": jnp.minimum(o + 1, n - 1)}
    to_l = {"outer": jnp.maximum(o - 1, 0)}
    has_r = o < n - 1
    has_l = o > 0

    loads = [
        pltpu.make_async_copy(
            partials.at[0, :, pl.ds(pl.multiple_of(i * half, half), half)], mine, loc.at[0]
        ),
        pltpu.make_async_copy(residual, resid, loc.at[1]),
        pltpu.make_async_copy(gain, gains, loc.at[2]),
        pltpu.make_async_copy(weight, w, loc.at[3]),
    ]

    def remote(src, dst, ssem, rsem, to):
        return pltpu.make_async_remote_copy(
            src_ref=src, dst_ref=dst, send_sem=ssem, recv_sem=rsem,
            device_id=to, device_id_type=MESH,
        )

    def y_copy(d, p):
        at = pl.multiple_of(other * half + d * local + p * cols, cols)
        return remote(partials.at[0, :, pl.ds(at, cols)], ybuf.at[d, p],
                      out_s.at[0], y_r.at[d, p], to_y)

    def r_copy(d, p):
        return remote(rbuf.at[d, p], rbuf.at[d, p], out_s.at[1], r_r.at[d, p], to_r)

    def l_copy(d, p):
        return remote(lbuf.at[d, p], lbuf.at[d, p], out_s.at[1], l_r.at[d, p], to_l)

    def g_copy(t, p, kind, to):
        k = t * pieces + p
        return remote(g.at[k], g.at[k], out_s.at[kind], g_r.at[k], to)

    def inside(p):
        return (p >= 0) & (p < pieces)

    def is_early(p):
        return lax.rem(p, CYCLE) < EARLY

    def level_one(d, p):
        y_copy(d, p).wait_recv()
        at = pl.multiple_of(d * local + p * cols, cols)
        return mine[:, pl.ds(at, cols)].astype(F32) + ybuf[d, p].astype(F32)

    def skew(d):
        return jnp.where(d > o, o, jnp.where(d < o, n - 1 - o, n - 1))

    def send_y(s):
        for d in range(n):
            p = s - skew(d)

            @pl.when(inside(p))
            def _():
                y_copy(d, p).start()

    barrier = pltpu.get_barrier_semaphore()
    pl.semaphore_signal(barrier, inc=1, device_id=to_y, device_id_type=MESH)

    @pl.when(has_r)
    def _():
        pl.semaphore_signal(barrier, inc=1, device_id=to_r, device_id_type=MESH)

    @pl.when(has_l)
    def _():
        pl.semaphore_signal(barrier, inc=1, device_id=to_l, device_id_type=MESH)

    for load in loads[:3]:
        load.start()
    pl.semaphore_wait(barrier, 1 + has_r.astype(jnp.int32) + has_l.astype(jnp.int32))
    for s in range(AHEAD):
        send_y(jnp.int32(s))
    loads[3].start()
    acc[...] = jnp.zeros_like(acc)
    sq[...] = jnp.zeros_like(sq)
    for load in loads[:3]:
        load.wait()

    def passing(s):
        p = s - o

        @pl.when(inside(p) & has_r)
        def _():
            for d in reversed(range(n)):
                @pl.when(d > o)
                def _():
                    value = level_one(d, p)

                    @pl.when(has_l)
                    def _():
                        r_copy(d, p).wait_recv()
                        rbuf[d, p] = (value + rbuf[d, p].astype(F32)).astype(BF16)

                    @pl.when(jnp.logical_not(has_l))
                    def _():
                        rbuf[d, p] = value.astype(BF16)

                    r_copy(d, p).start()

        q = s - (n - 1 - o)

        @pl.when(inside(q) & has_l)
        def _():
            for d in range(n):
                @pl.when(d < o)
                def _():
                    value = level_one(d, q)

                    @pl.when(has_r)
                    def _():
                        l_copy(d, q).wait_recv()
                        lbuf[d, q] = (value + lbuf[d, q].astype(F32)).astype(BF16)

                    @pl.when(jnp.logical_not(has_r))
                    def _():
                        lbuf[d, q] = value.astype(BF16)

                    l_copy(d, q).start()

    def finish(s):
        p = s - (n - 1)

        @pl.when(inside(p))
        def _():
            at = pl.multiple_of(p * cols, cols)
            tmp[...] = level_one(o, p) + resid[:, pl.ds(at, cols)].astype(F32)

            @pl.when(has_l)
            def _():
                r_copy(o, p).wait_recv()
                tmp[...] += rbuf[o, p].astype(F32)

            @pl.when(has_r)
            def _():
                l_copy(o, p).wait_recv()
                tmp[...] += lbuf[o, p].astype(F32)

            value = tmp[...].astype(BF16)
            stream_out[:, pl.ds(at, cols)] = value
            me = i * n + o
            g[me * pieces + p] = value

            @pl.when(is_early(p))
            def _():
                g_copy(me, p, 2, to_y).start()

    def along(c, t, p, kind):
        @pl.when((c <= o) & has_r)
        def _():
            g_copy(t, p, kind, to_r).start()

        @pl.when((c >= o) & has_l)
        def _():
            g_copy(t, p, kind, to_l).start()

    def near(s):
        for c in range(n):
            p = s - (n - 1) - jnp.abs(o - c)
            t = i * n + c

            @pl.when(inside(p))
            def _():
                @pl.when(c != o)
                def _():
                    g_copy(t, p, 3, to_r).wait_recv()

                along(c, t, p, 3)

                @pl.when(jnp.logical_not(is_early(p)))
                def _():
                    g_copy(t, p, 2, to_y).start()

    def far(s):
        for c in range(n):
            p = s - n - jnp.abs(o - c)
            t = other * n + c

            @pl.when(inside(p))
            def _():
                g_copy(t, p, 2, to_y).wait_recv()

                @pl.when(is_early(p))
                def _():
                    along(c, t, p, 4)

    def multiply(s):
        @pl.loop(0, 2 * n)
        def _(k):
            away = (k >= n).astype(jnp.int32)
            c = k - away * n
            p = s - (n - 1) - jnp.abs(o - c) - away
            t = jnp.where(away > 0, other, i) * n + c

            @pl.when(inside(p) & (lax.rem(p, group) == group - 1))
            def _():
                first = p - (group - 1)
                at = pl.multiple_of(t * local + first * cols, group * cols)
                parts = [g[t * pieces + first + j] for j in range(group)]
                value = jnp.concatenate(parts, axis=1).astype(F32)
                square = value * value
                part = square[:, :128]
                for j in range(1, group * cols // 128):
                    part += square[:, j * 128:(j + 1) * 128]
                sq[...] += part
                scaled = (value * gains[:, pl.ds(at, group * cols)]).astype(BF16)
                acc[...] += jnp.dot(
                    scaled, w[pl.ds(at, group * cols), :], preferred_element_type=F32
                )

    @pl.loop(0, pieces + 2 * n - 1)
    def _(s):
        send_y(s + AHEAD)
        passing(s)
        finish(s)
        near(s)
        far(s)

        @pl.when(s == n - 1)
        def _():
            loads[3].wait()

        multiply(s)

    factor = lax.rsqrt(jnp.sum(sq[...], axis=1, keepdims=True) / width + 1e-05)
    kv_out[...] = (acc[...] * factor).astype(BF16)

    def sent(ref, kind):
        remote(ref, ref, out_s.at[kind], g_r.at[0], to_y).wait_send()

    sent(ybuf, 0)
    sent(rbuf.at[pl.ds(0, n - 1)], 1)
    sent(g.at[pl.ds(0, n * (pieces - early) + early)], 2)

    @pl.when(has_l & has_r)
    def _():
        sent(g.at[pl.ds(0, (n + 1) * pieces)], 3)
        sent(g.at[pl.ds(0, (n + 1) * early)], 4)

    @pl.when(jnp.logical_not(has_l & has_r))
    def _():
        sent(g.at[pl.ds(0, pieces)], 3)
        sent(g.at[pl.ds(0, early)], 4)


def write_out(stream, kv, stream_out, kv_out, sems):
    copies = [
        pltpu.make_async_copy(stream, stream_out, sems.at[0]),
        pltpu.make_async_copy(kv, kv_out, sems.at[1]),
    ]
    for copy in copies:
        copy.start()
    for copy in copies:
        copy.wait()


def body(n, partials, residual, norm_gain, kv_weight):
    rows, local = residual.shape
    width = norm_gain.shape[0]
    heads_local, pair = kv_weight.shape[1:]
    pieces = PIECES
    cols = local // pieces
    wide = heads_local * pair
    dma = pltpu.SemaphoreType.DMA
    vmem = pltpu.VMEM
    stream, kv = pl.pallas_call(
        functools.partial(fused, n, pieces),
        out_shape=(
            jax.ShapeDtypeStruct((rows, local), BF16),
            jax.ShapeDtypeStruct((rows, wide), BF16),
        ),
        in_specs=[pl.BlockSpec(memory_space=pl.ANY)] * 4,
        out_specs=(pl.BlockSpec(memory_space=pltpu.VMEM),) * 2,
        scratch_shapes=[
            vmem((rows, n * local), BF16),
            vmem((rows, local), BF16),
            vmem((1, width), F32),
            vmem((width, wide), BF16),
            vmem((n, pieces, rows, cols), BF16),
            vmem((n, pieces, rows, cols), BF16),
            vmem((n, pieces, rows, cols), BF16),
            vmem((2 * n * pieces, rows, cols), BF16),
            vmem((rows, cols), F32),
            vmem((rows, wide), F32),
            vmem((rows, 128), F32),
            dma((4,)),
            dma((5,)),
            dma((n, pieces)),
            dma((n, pieces)),
            dma((n, pieces)),
            dma((2 * n * pieces,)),
        ],
        compiler_params=pltpu.CompilerParams(
            collective_id=0, has_side_effects=True, vmem_limit_bytes=60 * 1024 * 1024
        ),
        cost_estimate=pl.CostEstimate(
            flops=2 * rows * width * wide,
            bytes_accessed=2 * (rows * width + width * wide),
            transcendentals=rows,
        ),
    )(partials, residual, norm_gain.reshape(1, width), kv_weight.reshape(width, wide))
    stream, kv = pl.pallas_call(
        write_out,
        out_shape=(
            jax.ShapeDtypeStruct((rows, local), BF16),
            jax.ShapeDtypeStruct((rows, wide), BF16),
        ),
        in_specs=[pl.BlockSpec(memory_space=pl.ANY)] * 2,
        out_specs=(pl.BlockSpec(memory_space=pl.ANY),) * 2,
        scratch_shapes=[dma((2,))],
    )(stream, kv)
    return stream, kv.reshape(rows, heads_local, pair)


def solution(mesh):
    placed = (
        P(("dp", "inner", "outer"), None, None),
        P("dp", ("inner", "outer")),
        P(),
        P(None, ("inner", "outer"), None),
    )
    return jax.shard_map(
        functools.partial(body, mesh.shape["outer"]),
        mesh=mesh,
        in_specs=placed,
        out_specs=(P("dp", ("inner", "outer")), P("dp", ("inner", "outer"), None)),
        check_vma=False,
    )
```

```python
import functools

import jax
import jax.numpy as jnp
from jax import lax
from jax.experimental import pallas as pl
from jax.experimental.pallas import tpu as pltpu
from jax.sharding import PartitionSpec as P

MESH = pl.DeviceIdType.MESH
F32 = jnp.float32
BF16 = jnp.bfloat16
PIECES = 8
AHEAD = 2
CYCLE = 2
EARLY = 1


def fused(n, pieces, partials, residual, gain, weight, stream_out, kv_out,
          mine, resid, gains, w, ybuf, rbuf, lbuf, g, tmp, acc, sq,
          loc, out_s, y_r, r_r, l_r, g_r):
    i = lax.axis_index("inner")
    o = lax.axis_index("outer")
    other = 1 - i
    rows, local = resid.shape
    width = gains.shape[1]
    half = n * local
    cols = local // pieces
    group = max(1, 256 // cols)
    early = sum(p % CYCLE < EARLY for p in range(pieces))
    to_y = {"inner": other}
    to_r = {"outer": jnp.minimum(o + 1, n - 1)}
    to_l = {"outer": jnp.maximum(o - 1, 0)}
    has_r = o < n - 1
    has_l = o > 0

    loads = [
        pltpu.make_async_copy(
            partials.at[0, :, pl.ds(pl.multiple_of(i * half, half), half)], mine, loc.at[0]
        ),
        pltpu.make_async_copy(residual, resid, loc.at[1]),
        pltpu.make_async_copy(gain, gains, loc.at[2]),
        pltpu.make_async_copy(weight, w, loc.at[3]),
    ]

    def remote(src, dst, ssem, rsem, to):
        return pltpu.make_async_remote_copy(
            src_ref=src, dst_ref=dst, send_sem=ssem, recv_sem=rsem,
            device_id=to, device_id_type=MESH,
        )

    def y_copy(d, p):
        at = pl.multiple_of(other * half + d * local + p * cols, cols)
        return remote(partials.at[0, :, pl.ds(at, cols)], ybuf.at[d, p],
                      out_s.at[0], y_r.at[d, p], to_y)

    def r_copy(d, p):
        return remote(rbuf.at[d, p], rbuf.at[d, p], out_s.at[1], r_r.at[d, p], to_r)

    def l_copy(d, p):
        return remote(lbuf.at[d, p], lbuf.at[d, p], out_s.at[1], l_r.at[d, p], to_l)

    def g_copy(t, p, kind, to):
        k = t * pieces + p
        return remote(g.at[k], g.at[k], out_s.at[kind], g_r.at[k], to)

    def inside(p):
        return (p >= 0) & (p < pieces)

    def is_early(p):
        return lax.rem(p, CYCLE) < EARLY

    def level_one(d, p):
        y_copy(d, p).wait_recv()
        at = pl.multiple_of(d * local + p * cols, cols)
        return mine[:, pl.ds(at, cols)].astype(F32) + ybuf[d, p].astype(F32)

    def skew(d):
        return jnp.where(d > o, o, jnp.where(d < o, n - 1 - o, n - 1))

    def send_y(s):
        for d in range(n):
            p = s - skew(d)

            @pl.when(inside(p))
            def _():
                y_copy(d, p).start()

    barrier = pltpu.get_barrier_semaphore()
    pl.semaphore_signal(barrier, inc=1, device_id=to_y, device_id_type=MESH)

    @pl.when(has_r)
    def _():
        pl.semaphore_signal(barrier, inc=1, device_id=to_r, device_id_type=MESH)

    @pl.when(has_l)
    def _():
        pl.semaphore_signal(barrier, inc=1, device_id=to_l, device_id_type=MESH)

    for load in loads[:3]:
        load.start()
    pl.semaphore_wait(barrier, 1 + has_r.astype(jnp.int32) + has_l.astype(jnp.int32))
    for s in range(AHEAD):
        send_y(jnp.int32(s))
    loads[3].start()
    acc[...] = jnp.zeros_like(acc)
    sq[...] = jnp.zeros_like(sq)
    for load in loads[:3]:
        load.wait()

    def passing(s):
        p = s - o

        @pl.when(inside(p) & has_r)
        def _():
            for d in reversed(range(n)):
                @pl.when(d > o)
                def _():
                    value = level_one(d, p)

                    @pl.when(has_l)
                    def _():
                        r_copy(d, p).wait_recv()
                        rbuf[d, p] = (value + rbuf[d, p].astype(F32)).astype(BF16)

                    @pl.when(jnp.logical_not(has_l))
                    def _():
                        rbuf[d, p] = value.astype(BF16)

                    r_copy(d, p).start()

        q = s - (n - 1 - o)

        @pl.when(inside(q) & has_l)
        def _():
            for d in range(n):
                @pl.when(d < o)
                def _():
                    value = level_one(d, q)

                    @pl.when(has_r)
                    def _():
                        l_copy(d, q).wait_recv()
                        lbuf[d, q] = (value + lbuf[d, q].astype(F32)).astype(BF16)

                    @pl.when(jnp.logical_not(has_r))
                    def _():
                        lbuf[d, q] = value.astype(BF16)

                    l_copy(d, q).start()

    def finish(s):
        p = s - (n - 1)

        @pl.when(inside(p))
        def _():
            at = pl.multiple_of(p * cols, cols)
            tmp[...] = level_one(o, p) + resid[:, pl.ds(at, cols)].astype(F32)

            @pl.when(has_l)
            def _():
                r_copy(o, p).wait_recv()
                tmp[...] += rbuf[o, p].astype(F32)

            @pl.when(has_r)
            def _():
                l_copy(o, p).wait_recv()
                tmp[...] += lbuf[o, p].astype(F32)

            value = tmp[...].astype(BF16)
            stream_out[:, pl.ds(at, cols)] = value
            me = i * n + o
            g[me * pieces + p] = value

            @pl.when(is_early(p))
            def _():
                g_copy(me, p, 2, to_y).start()

    def along(c, t, p, kind):
        @pl.when((c <= o) & has_r)
        def _():
            g_copy(t, p, kind, to_r).start()

        @pl.when((c >= o) & has_l)
        def _():
            g_copy(t, p, kind, to_l).start()

    def near(s):
        for c in range(n):
            p = s - (n - 1) - jnp.abs(o - c)
            t = i * n + c

            @pl.when(inside(p))
            def _():
                @pl.when(c != o)
                def _():
                    g_copy(t, p, 3, to_r).wait_recv()

                along(c, t, p, 3)

                @pl.when(jnp.logical_not(is_early(p)))
                def _():
                    g_copy(t, p, 2, to_y).start()

    def far(s):
        for c in range(n):
            p = s - n - jnp.abs(o - c)
            t = other * n + c

            @pl.when(inside(p))
            def _():
                g_copy(t, p, 2, to_y).wait_recv()

                @pl.when(is_early(p))
                def _():
                    along(c, t, p, 4)

    def multiply(s):
        @pl.loop(0, 2 * n)
        def _(k):
            away = (k >= n).astype(jnp.int32)
            c = k - away * n
            p = s - (n - 1) - jnp.abs(o - c) - away
            t = jnp.where(away > 0, other, i) * n + c

            @pl.when(inside(p) & (lax.rem(p, group) == group - 1))
            def _():
                first = p - (group - 1)
                at = pl.multiple_of(t * local + first * cols, group * cols)
                parts = [g[t * pieces + first + j] for j in range(group)]
                value = jnp.concatenate(parts, axis=1).astype(F32)
                square = value * value
                part = square[:, :128]
                for j in range(1, group * cols // 128):
                    part += square[:, j * 128:(j + 1) * 128]
                sq[...] += part
                scaled = (value * gains[:, pl.ds(at, group * cols)]).astype(BF16)
                acc[...] += jnp.dot(
                    scaled, w[pl.ds(at, group * cols), :], preferred_element_type=F32
                )

    @pl.loop(0, pieces + 2 * n - 1)
    def _(s):
        send_y(s + AHEAD)
        passing(s)
        finish(s)
        near(s)
        far(s)

        @pl.when(s == n - 1)
        def _():
            loads[3].wait()

        multiply(s)

    factor = lax.rsqrt(jnp.sum(sq[...], axis=1, keepdims=True) / width + 1e-05)
    kv_out[...] = (acc[...] * factor).astype(BF16)

    def sent(ref, kind):
        remote(ref, ref, out_s.at[kind], g_r.at[0], to_y).wait_send()

    sent(ybuf, 0)
    sent(rbuf.at[pl.ds(0, n - 1)], 1)
    sent(g.at[pl.ds(0, n * (pieces - early) + early)], 2)

    @pl.when(has_l & has_r)
    def _():
        sent(g.at[pl.ds(0, (n + 1) * pieces)], 3)
        sent(g.at[pl.ds(0, (n + 1) * early)], 4)

    @pl.when(jnp.logical_not(has_l & has_r))
    def _():
        sent(g.at[pl.ds(0, pieces)], 3)
        sent(g.at[pl.ds(0, early)], 4)


def body(n, partials, residual, norm_gain, kv_weight):
    rows, local = residual.shape
    width = norm_gain.shape[0]
    heads_local, pair = kv_weight.shape[1:]
    pieces = PIECES
    cols = local // pieces
    wide = heads_local * pair
    dma = pltpu.SemaphoreType.DMA
    vmem = pltpu.VMEM
    stream, kv = pl.pallas_call(
        functools.partial(fused, n, pieces),
        out_shape=(
            jax.ShapeDtypeStruct((rows, local), BF16),
            jax.ShapeDtypeStruct((rows, wide), BF16),
        ),
        in_specs=[pl.BlockSpec(memory_space=pl.ANY)] * 4,
        out_specs=(pl.BlockSpec(memory_space=pltpu.VMEM),) * 2,
        scratch_shapes=[
            vmem((rows, n * local), BF16),
            vmem((rows, local), BF16),
            vmem((1, width), F32),
            vmem((width, wide), BF16),
            vmem((n, pieces, rows, cols), BF16),
            vmem((n, pieces, rows, cols), BF16),
            vmem((n, pieces, rows, cols), BF16),
            vmem((2 * n * pieces, rows, cols), BF16),
            vmem((rows, cols), F32),
            vmem((rows, wide), F32),
            vmem((rows, 128), F32),
            dma((4,)),
            dma((5,)),
            dma((n, pieces)),
            dma((n, pieces)),
            dma((n, pieces)),
            dma((2 * n * pieces,)),
        ],
        compiler_params=pltpu.CompilerParams(
            collective_id=0, has_side_effects=True, vmem_limit_bytes=60 * 1024 * 1024
        ),
        cost_estimate=pl.CostEstimate(
            flops=2 * rows * width * wide,
            bytes_accessed=2 * (rows * width + width * wide),
            transcendentals=rows,
        ),
    )(partials, residual, norm_gain.reshape(1, width), kv_weight.reshape(width, wide))
    return stream, kv.reshape(rows, heads_local, pair)


def solution(mesh):
    placed = (
        P(("dp", "inner", "outer"), None, None),
        P("dp", ("inner", "outer")),
        P(),
        P(None, ("inner", "outer"), None),
    )
    return jax.shard_map(
        functools.partial(body, mesh.shape["outer"]),
        mesh=mesh,
        in_specs=placed,
        out_specs=(P("dp", ("inner", "outer")), P("dp", ("inner", "outer"), None)),
        check_vma=False,
    )
```
